128 devices in a mesh: term: 8 (over x, core), sector: 16 (over z, y).
Axes of the slice: x: 4, y: 4, z: 4, core: 2. Of those that a mesh axis runs over, the one named last changes fastest.
Arguments:
- start_vector: float32 [16, 384, 384], P('sector')
- precond: float32 [16, 384, 384], P('sector'), may hold values from 0.5 to 4
- op_left: bfloat16 [8, 16, 12, 384, 384], P('term', 'sector'), may hold values from -0.03125 to 0.03125
- op_right: bfloat16 [8, 16, 12, 384, 384], P('term', 'sector'), may hold values from -0.3125 to 0.3125
- slot_source: int32 [8, 16, 12], P('term', 'sector'), may hold values from 0 to 15
- slot_count: int32 [8, 16], P('term', 'sector'), may hold values from 1 to 12, as said below
Outputs:
- final_vector: float32 [16, 384, 384], P('sector')
- ritz: float32 [4], replicated
The draws below stay inside these ranges and needn't reach their ends.
Inputs may be any that keep to these rules, and one draw needn't show every extreme that they name: `slot_count`: each entry is one live count; some term group and sector has exactly 12 live slots.
All inputs are finite; a program needn't handle non-finite values.
Results may differ from the reference program's by a relative error of at most 0.025.
Values may be sent and summed in bfloat16 or wider, within the bound.
No kernel may reach another device: no remote copies, remote signals or barrier semaphores. Data moves between devices by JAX's collectives and lax.ppermute only.
A program may use at most 64 MiB of HBM per device.

```python
import math
import jax
import jax.numpy as jnp
from jax import lax

M = 384
SLOTS = 12
ITERS = 4
SECTORS = 16
N_TERM = 8


def draw_start_vector(key, part):
    key = jax.random.fold_in(key, 7)
    noise_key, row_key, col_key = jax.random.split(key, 3)
    sector_pos = jnp.arange(SECTORS, dtype=jnp.float32).reshape(SECTORS, 1, 1)
    sector_ramp = jnp.exp(math.log(3.0) * sector_pos / max(SECTORS - 1, 1))
    row_scale = jnp.exp(jax.random.uniform(row_key, (SECTORS, M, 1), jnp.float32, 0.0, math.log(10.0)))
    col_scale = jnp.exp(jax.random.uniform(col_key, (SECTORS, 1, M), jnp.float32, 0.0, math.log(10.0)))
    base = jnp.clip(jax.random.normal(noise_key, (SECTORS, M, M), jnp.float32), -4.0, 4.0)
    return base * row_scale * col_scale * sector_ramp


def draw_slot_count(key, part):
    key = jax.random.fold_in(key, 13)
    first_key, second_key, pick_key = jax.random.split(key, 3)
    grid_shape = (N_TERM, SECTORS)
    first_draw = jax.random.randint(first_key, grid_shape, 0, SLOTS)
    second_draw = jax.random.randint(second_key, grid_shape, 0, SLOTS)
    counts = 1 + first_draw * second_draw // SLOTS
    chosen = jax.random.randint(pick_key, (), 0, N_TERM * SECTORS)
    position = jnp.arange(N_TERM * SECTORS, dtype=jnp.int32).reshape(grid_shape)
    return jnp.where(position == chosen, SLOTS, counts).astype(jnp.int32)


def touch_ends(values, stream_key, low, high):
    longest = values.shape.index(max(values.shape))
    spots = []
    for shift in (0, 1):
        where = [jax.random.randint(jax.random.fold_in(stream_key, axis), (), 0, length) for axis, length in enumerate(values.shape)]
        where[longest] = (where[longest] + shift) % values.shape[longest]
        spots.append(tuple(where))
    return values.at[spots[0]].set(low).at[spots[1]].set(high)


def levels(key, dims, cuts, low, largest):
    def one(dim, blocks):
        heights = jax.random.uniform(jax.random.fold_in(jax.random.fold_in(key, 6), dim), (blocks,), jnp.float32, low / len(cuts), largest / len(cuts))
        return jnp.repeat(jnp.exp(heights), dims[dim] // blocks).reshape((-1,) + (1,) * (len(dims) - dim - 1))

    loudness = one(*cuts[0])
    for cut in cuts[1:]:
        loudness = loudness * one(*cut)
    return loudness


def noise(stream_key, shape, scale, most, cuts=(), kind=jnp.bfloat16):
    loudness = levels(stream_key, shape, cuts, -0.22, 0.18) if cuts else 1.0
    values = jax.random.normal(stream_key, shape, jnp.float32) * scale * loudness
    return jnp.minimum(jnp.maximum(values, -most), most).astype(kind)


def setup_inputs(seed: int = 0) -> dict:
    keys = jax.random.split(jax.random.key(seed), 7)
    start_vector = draw_start_vector(jax.random.fold_in(keys[6], 71), 0)
    precond = jnp.clip(jnp.exp(math.log(4.0) - 2.0794415 * jax.random.uniform(keys[1], (SECTORS, M, M), jnp.float32) ** levels(keys[1], (SECTORS, M, M), ((0, 16),), -0.2, 0.2)), 0.5, 4.0)
    op_left = noise(keys[2], (N_TERM, SECTORS, SLOTS, M, M), (M * N_TERM * SLOTS) ** -0.5, 0.03125, ((0, 8), (1, 16)))
    op_right = noise(keys[3], (N_TERM, SECTORS, SLOTS, M, M), M ** -0.5, 0.3125, ((0, 8), (1, 16)))
    slot_source = touch_ends(jax.random.randint(keys[4], (N_TERM, SECTORS, SLOTS), 0, SECTORS), jax.random.fold_in(keys[4], 1), 0, SECTORS - 1).astype(jnp.int32)
    slot_count = draw_slot_count(jax.random.fold_in(keys[6], 71), 0)
    return dict(start_vector=start_vector, precond=precond, op_left=op_left, op_right=op_right, slot_source=slot_source, slot_count=slot_count)


EPS = 1e-06
HIGHEST = lax.Precision.HIGHEST

def apply_operator(field, op_left, op_right, slot_source, slot_count):
    rounded = field.astype(jnp.bfloat16)
    widened = rounded.astype(jnp.float32)
    slot_ids = jnp.arange(SLOTS, dtype=jnp.int32)
    live_mask = (slot_ids[None, None, :] < slot_count[:, :, None]).astype(jnp.float32)

    def one_group(summed, pieces):
        left_ops, right_ops, sources, mask_rows = pieces
        chosen = widened[sources]
        product = jnp.einsum('klij,kljm->klim', left_ops.astype(jnp.float32), chosen, precision=HIGHEST)
        product = lax.optimization_barrier(product.astype(jnp.bfloat16))
        contrib = jnp.einsum('klim,klnm->klin', product.astype(jnp.float32), right_ops.astype(jnp.float32), precision=HIGHEST)
        return (summed + lax.optimization_barrier(jnp.sum(contrib * mask_rows[:, :, None, None], axis=1)), None)
    summed, _ = lax.scan(one_group, jnp.zeros(field.shape, jnp.float32), (op_left, op_right, slot_source, live_mask))
    return summed

def reference(start_vector, precond, op_left, op_right, slot_source, slot_count):
    entries = float(SECTORS * M * M)

    def mean_of(values):
        return jnp.sum(values) / entries

    def apply_field(field):
        return apply_operator(field, op_left, op_right, slot_source, slot_count)
    vector = start_vector / jnp.sqrt(mean_of(start_vector * start_vector) + EPS)
    image = apply_field(vector)
    theta = mean_of(vector * image)
    ritz_values = []
    for iteration in range(ITERS):
        direct = (image - theta * vector) / precond
        along = mean_of(vector * direct)
        direct = direct - along * vector
        trial = direct / jnp.sqrt(mean_of(direct * direct) + EPS)
        result = apply_field(trial)
        left_mix = mean_of(vector * result)
        right_mix = mean_of(trial * image)
        corner = mean_of(trial * result)
        coupling = 0.5 * (left_mix + right_mix)
        lowest = 0.5 * (theta + corner) - jnp.sqrt((0.5 * (theta - corner)) ** 2 + coupling * coupling)
        ritz_values.append(lowest)
        weight_old = corner - lowest
        fresh = weight_old * vector - coupling * trial
        fresh_image = weight_old * image - coupling * result
        factor = 1.0 / jnp.sqrt(mean_of(fresh * fresh) + EPS)
        vector = fresh * factor
        image = fresh_image * factor
        theta = mean_of(vector * image)
    return (vector, jnp.stack(ritz_values))
```

```python
import functools

import jax
import jax.numpy as jnp
from jax import lax
from jax.experimental import pallas as pl
from jax.experimental.pallas import tpu as pltpu
from jax.sharding import PartitionSpec as P


ITERS = 4
EPS = 1e-6
W = 384
HALF = W // 2
PART = HALF // 2
SC = 16
SECTORS = 16
ENTRIES = float(SECTORS * W * W)
ORDER = {0: 0, 1: 1, 3: 2, 2: 3}
F32 = jnp.float32
BF16 = jnp.bfloat16
VM = pl.BlockSpec(memory_space=pltpu.VMEM)
SM = pl.BlockSpec(memory_space=pltpu.SMEM)
PARAMS = pltpu.CompilerParams(vmem_limit_bytes=16 * 1024 * 1024)


def kernel_call(body, out_shape, in_specs, scratch=(), aliases=None):
    call = pl.pallas_call(
        body,
        out_shape=jax.tree.map(lambda s: pltpu.VMEM(s.shape, s.dtype), out_shape),
        in_specs=in_specs,
        out_specs=jax.tree.map(lambda _: VM, out_shape),
        scratch_shapes=scratch,
        input_output_aliases=aliases or {},
        compiler_params=PARAMS,
    )

    def run(*operands):
        placed = [
            pltpu.with_memory_space_constraint(x, pltpu.VMEM) if spec is VM else x
            for x, spec in zip(operands, in_specs)
        ]
        return call(*placed)

    return run


def triple(values):
    tall = jnp.concatenate(
        [jnp.broadcast_to(v, (1, 128)) for v in values] + [jnp.zeros((SC - len(values), 128), F32)], axis=0
    )
    high = tall.astype(BF16)
    rest = tall - high.astype(F32)
    mid = rest.astype(BF16)
    low = (rest - mid.astype(F32)).astype(BF16)
    return jnp.concatenate([high, mid, low], axis=1)


def sums_of(tile):
    tall = tile[:, 0:128] + tile[:, 128:256] + tile[:, 256:384]
    return [tall[k : k + 1, 0:1] for k in range(8)]


def total(x):
    return jnp.sum(jnp.sum(x, axis=0, keepdims=True), axis=1, keepdims=True)


def piece(groups, r, stride, part):
    rz, ry = r >> 2, r & 3
    outer, inner = (rz, ry) if part == 0 else (ry, rz)
    own, one, three, two_low, two_high = groups
    at = ORDER[inner]
    if outer == 2:
        return (two_low, at * stride) if at < 2 else (two_high, (at - 2) * stride)
    return {0: own, 1: one, 3: three}[outer], at * stride


def tree_sum(tiles):
    for bit in (1, 2, 4, 8):
        tiles = {r: t + tiles[r ^ bit] for r, t in tiles.items() if not r & bit}
    return tiles[0]


def sector_sums(groups_a, stride):
    tiles = {}
    for r in range(SECTORS):
        ref, row = piece(groups_a, r, stride, 0)
        tiles[r] = ref[row + PART : row + PART + SC, :].astype(F32)
    return sums_of(tree_sum(tiles))


def prep_kernel(core, start, precond, x_own, q_own, msg_a, msg_b, xt, qt):
    c = core[0]
    xt[...] = jnp.transpose(start[...])
    qt[...] = 1.0 / jnp.transpose(precond[...])
    here, there = pl.multiple_of(c * HALF, HALF), pl.multiple_of((1 - c) * HALF, HALF)
    x_own[0:HALF, :] = xt[pl.ds(here, HALF), :]
    x_own[HALF:W, :] = xt[pl.ds(there, HALF), :]
    q_own[0:HALF, :] = qt[pl.ds(here, HALF), :]
    q_own[HALF:W, :] = qt[pl.ds(there, HALF), :]
    x = x_own[...]
    msg_a[0:PART, :] = x[0:PART].astype(BF16)
    msg_a[PART : PART + SC, :] = triple([total(x * x)])
    msg_a[PART + SC : 2 * PART + SC, :] = q_own[0:PART, :].astype(BF16)
    msg_b[0:PART, :] = x[PART:HALF].astype(BF16)
    msg_b[PART : 2 * PART, :] = q_own[PART:HALF, :].astype(BF16)


def contract(tables, ops, xs, acc):
    acc[...] = jnp.zeros_like(acc)
    for (pos, count), (left, right) in zip(tables, ops):

        def slot(j, carry):
            product = lax.dot_general(
                xs[pos[j]], left[j], (((1,), (1,)), ((), ())), preferred_element_type=F32
            ).astype(BF16)
            acc[...] += jnp.dot(right[j], product, preferred_element_type=F32)
            return carry

        lax.fori_loop(0, count[0], slot, 0)


def emit(c, acc, v_own, d_own, known, keep, send):
    here, there = pl.multiple_of(c * HALF, HALF), pl.multiple_of((1 - c) * HALF, HALF)
    mine, other = acc[pl.ds(here, HALF), :], acc[pl.ds(there, HALF), :]
    keep[...] = mine
    vz = total(v_own[0:HALF, :] * mine + v_own[HALF:W, :] * other)
    if d_own is None:
        values = [vz]
    else:
        values = [vz, total(d_own[0:HALF, :] * mine + d_own[HALF:W, :] * other)] + [k * 0.125 for k in known]
    send[0:HALF, :] = other.astype(BF16)
    send[HALF : HALF + SC, :] = triple(values)


def first_kernel(*refs):
    core, pos, count, pos2, count2 = refs[:5]
    groups_a, groups_b = refs[5:10], refs[10:15]
    x_own, left, right, left2, right2 = refs[15:20]
    state, v_own, v, q, xs, keep, send, acc = refs[20:]
    norm = sector_sums(groups_a, 2 * PART + SC)[0] / ENTRIES
    scale = 1.0 / jnp.sqrt(norm + EPS)
    state[0:1, :] = jnp.broadcast_to(norm * scale * scale, (1, 128))
    state[1:8, :] = jnp.zeros((7, 128), F32)
    v_own[...] = x_own[...] * scale
    for r in range(SECTORS):
        for part, groups, stride, skip in ((0, groups_a, 2 * PART + SC, SC), (1, groups_b, 2 * PART, 0)):
            ref, row = piece(groups, r, stride, part)
            at = slice(part * PART, part * PART + PART)
            vector = ref[row : row + PART, :].astype(F32) * scale
            v[r, at, :] = vector
            xs[r, at, :] = vector.astype(BF16)
            q[r, at, :] = ref[row + PART + skip : row + 2 * PART + skip, :]
    contract(((pos, count), (pos2, count2)), ((left, right), (left2, right2)), xs, acc)
    emit(core[0], acc, v_own, None, None, keep, send)


def step_scalars(state, sums):
    vz, dz, vd, dd, dw = [s / ENTRIES for s in sums[:5]]
    vv, vw = state[0:1, 0:1], state[1:2, 0:1]
    along = vd
    inverse = 1.0 / jnp.sqrt(dd - 2.0 * along * vd + along * along * vv + EPS)
    left = inverse * (vz - along * vw)
    right = inverse * (dw - along * vw)
    corner = inverse * inverse * (dz - along * (vz + dw) + along * along * vw)
    coupling = 0.5 * (left + right)
    half_gap = 0.5 * (vw - corner)
    ritz = 0.5 * (vw + corner) - jnp.sqrt(half_gap * half_gap + coupling * coupling)
    weight_old = corner - ritz
    alpha = weight_old + coupling * inverse * along
    beta = -coupling * inverse
    norm = alpha * alpha * vv + 2.0 * alpha * beta * vd + beta * beta * dd
    factor = 1.0 / jnp.sqrt(norm + EPS)
    alpha, beta = alpha * factor, beta * factor
    new_vv = norm * factor * factor
    theta = alpha * alpha * vw + alpha * beta * (vz + dw) + beta * beta * dz
    return alpha, beta, new_vv, theta, ritz


def step_kernel(iteration, *refs):
    core, pos, count, pos2, count2 = refs[:5]
    groups_a, groups_b = refs[5:10], refs[10:15]
    other_z, old_state, old_v_own, old_w_own, old_d_own, q_own = refs[15:21]
    old_v, old_w, q, old_xs, left, right, left2, right2 = refs[21:29]
    state, v_own, w_own, d_own, v, w, xs, keep, send, acc = refs[29:]
    first = iteration == 0
    stride = PART + SC
    sums = sector_sums(groups_a, stride)
    own_z = jnp.concatenate(
        [
            groups_a[0][0:PART, :],
            groups_b[0][0:PART, :],
            other_z[0:PART, :],
            other_z[PART + SC : 2 * PART + SC, :],
        ],
        axis=0,
    ).astype(F32)
    state[...] = old_state[...]
    if first:
        theta = sums[0] / ENTRIES
        v_o, w_o = old_v_own[...], own_z
    else:
        alpha, beta, new_vv, theta, ritz = step_scalars(old_state, sums)
        state[0:1, :] = jnp.broadcast_to(new_vv, (1, 128))
        state[3 + iteration : 4 + iteration, :] = jnp.broadcast_to(ritz, (1, 128))
        v_o = alpha * old_v_own[...] + beta * old_d_own[...]
        w_o = alpha * old_w_own[...] + beta * own_z
    state[1:2, :] = jnp.broadcast_to(theta, (1, 128))
    d_o = (w_o - theta * v_o) * q_own[...]
    v_own[...] = v_o
    w_own[...] = w_o
    d_own[...] = d_o
    known = [total(v_o * d_o), total(d_o * d_o), total(d_o * w_o)]
    for r in range(SECTORS):
        for part, groups, step in ((0, groups_a, stride), (1, groups_b, PART)):
            ref, row = piece(groups, r, step, part)
            at = slice(part * PART, part * PART + PART)
            z = ref[row : row + PART, :].astype(F32)
            if first:
                vector, image = old_v[r, at, :], z
            else:
                vector = alpha * old_v[r, at, :] + beta * old_xs[r, at, :].astype(F32)
                image = alpha * old_w[r, at, :] + beta * z
            v[r, at, :] = vector
            w[r, at, :] = image
            xs[r, at, :] = ((image - theta * vector) * q[r, at, :].astype(F32)).astype(BF16)
    contract(((pos, count), (pos2, count2)), ((left, right), (left2, right2)), xs, acc)
    emit(core[0], acc, v_own, d_own, known, keep, send)


def pair_kernel(keep, send, came, out):
    out[0:HALF, :] = (keep[...] + came[0:HALF, :].astype(F32)).astype(BF16)
    mine, other = send[HALF : HALF + SC, :].astype(F32), came[HALF : HALF + SC, :].astype(F32)
    out[HALF : HALF + SC, :] = triple(sums_of(mine + other))


def chips_kernel(own, one, two, three, out, msg_a, msg_b):
    z = (own[...].astype(F32) + one[...].astype(F32)) + (two[...].astype(F32) + three[...].astype(F32))
    block = z[0:HALF].astype(BF16)
    tile = triple(sums_of(z[HALF : HALF + SC]))
    msg_a[0:PART, :] = block[0:PART]
    msg_a[PART : PART + SC, :] = tile
    msg_b[...] = block[PART:HALF]
    out[0:PART, :] = block[0:PART]
    out[PART : PART + SC, :] = tile
    out[PART + SC : 2 * PART + SC, :] = block[PART:HALF]


def last_kernel(core, one, two, three, own, old_state, v_own, d_own, vector, ritz, turned):
    c = core[0]
    tiles = (own[...] + one[...]) + (two[...] + three[...])
    alpha, beta, _, _, lowest = step_scalars(old_state, sums_of(tiles))
    ritz[...] = old_state[...]
    ritz[3 + ITERS : 4 + ITERS, :] = jnp.broadcast_to(lowest, (1, 128))
    here, there = pl.multiple_of(c * HALF, HALF), pl.multiple_of((1 - c) * HALF, HALF)
    turned[pl.ds(here, HALF), :] = alpha * v_own[0:HALF, :] + beta * d_own[0:HALF, :]
    turned[pl.ds(there, HALF), :] = alpha * v_own[HALF:W, :] + beta * d_own[HALF:W, :]
    vector[...] = jnp.transpose(turned[...])


def shape(*dims, dtype=F32):
    return jax.ShapeDtypeStruct(dims, dtype)


def xor(axis, mask):
    return lambda x: lax.ppermute(x, axis, [(i, i ^ mask) for i in range(lax.axis_size(axis))])


def gather_blocks(msg_a, msg_b):
    y1, y2, y3 = (xor("sector", m) for m in (1, 2, 3))
    z1, z2, z3 = (xor("sector", 4 * m) for m in (1, 2, 3))

    def part(msg, along, across):
        (n1, n2, n3), (m1, m3) = along, across
        own = jnp.concatenate([msg, n1(msg), n3(msg), n2(msg)], axis=0)
        one, three = m1(own), m3(own)
        cut = 2 * msg.shape[0]
        return own, one, three, m1(three[:cut]), m3(one[cut:])

    return part(msg_a, (y1, y2, y3), (z1, z3)), part(msg_b, (z1, z2, z3), (y1, y3))


def shards(start_vector, precond, op_left, op_right, slot_source, slot_count):
    left, right = op_left[0, 0], op_right[0, 0]
    slots = left.shape[0]
    me = lax.axis_index("sector")
    c = lax.axis_index("term") % 2
    core = c[None].astype(jnp.int32)
    pair = xor("term", 1)
    chip1, chip2, chip3 = (xor("term", 2 * m) for m in (1, 2, 3))

    table = jnp.concatenate([slot_source[0, 0] ^ me, slot_count[0]])
    table2 = pair(table)
    tables = (table[:slots], table[slots:], table2[:slots], table2[slots:])
    low, high = right[:, :, :HALF], right[:, :, HALF:]
    right_here = jnp.where(c == 0, low, high)
    right2 = pair(jnp.where(c == 0, high, low))
    left2 = pair(left)
    ops = (left, right_here, left2, right2)

    x_own, q_own, msg_a, msg_b = kernel_call(
        prep_kernel,
        [shape(W, W), shape(W, W), shape(2 * PART + SC, W, dtype=BF16), shape(2 * PART, W, dtype=BF16)],
        [SM, VM, VM],
        [pltpu.VMEM((W, W), F32)] * 2,
    )(core, start_vector[0], precond[0])
    groups_a, groups_b = gather_blocks(msg_a, msg_b)

    field = functools.partial(shape, SECTORS, HALF, W)
    outs = [shape(HALF, W), shape(HALF + SC, W, dtype=BF16)]
    acc = [pltpu.VMEM((W, W), F32)]
    state, v_own, v, q, xs, keep, send = kernel_call(
        first_kernel,
        [shape(8, 128), shape(W, W), field(), field(dtype=BF16), field(dtype=BF16)] + outs,
        [SM] * 5 + [VM] * 15,
        acc,
    )(core, *tables, *groups_a, *groups_b, x_own, *ops)
    w, w_own, d_own = v, v_own, v_own

    for iteration in range(ITERS):
        came = pair(send)
        both = kernel_call(pair_kernel, shape(HALF + SC, W, dtype=BF16), [VM] * 3)(keep, send, came)
        block, msg_a, msg_b = kernel_call(
            chips_kernel,
            [
                shape(HALF + SC, W, dtype=BF16),
                shape(PART + SC, W, dtype=BF16),
                shape(PART, W, dtype=BF16),
            ],
            [VM] * 4,
        )(both, chip1(both), chip2(both), chip3(both))
        other_z = pair(block)
        groups_a, groups_b = gather_blocks(msg_a, msg_b)
        state, v_own, w_own, d_own, v, w, xs, keep, send = kernel_call(
            functools.partial(step_kernel, iteration),
            [shape(8, 128), shape(W, W), shape(W, W), shape(W, W), field(), field(), field(dtype=BF16)] + outs,
            [SM] * 5 + [VM] * 24,
            acc,
            {16: 0, 21: 4, 24: 6} if iteration == 0 else {16: 0, 17: 1, 18: 2, 19: 3, 21: 4, 22: 5, 24: 6},
        )(
            core, *tables, *groups_a, *groups_b, other_z, state, v_own, w_own, d_own, q_own, v, w, q, xs, *ops
        )

    tile = send[HALF:].astype(F32)
    tile = tile + pair(tile)
    tile = (tile + chip1(tile)) + (chip2(tile) + chip3(tile))
    y1, y2, y3 = (xor("sector", m) for m in (1, 2, 3))
    z1, z2, z3 = (xor("sector", 4 * m) for m in (1, 2, 3))
    tile = (tile + y1(tile)) + (y2(tile) + y3(tile))
    vector, ritz = kernel_call(
        last_kernel,
        [shape(W, W), shape(8, 128)],
        [SM] + [VM] * 7,
        [pltpu.VMEM((W, W), F32)],
    )(core, z1(tile), z2(tile), z3(tile), tile, state, v_own, d_own)
    return vector[None], ritz[8 - ITERS :, 0]


def solution(mesh):
    in_specs = (
        P("sector", None, None),
        P("sector", None, None),
        P("term", "sector", None, None, None),
        P("term", "sector", None, None, None),
        P("term", "sector", None),
        P("term", "sector"),
    )
    out_specs = (P("sector", None, None), P())
    return jax.shard_map(shards, mesh=mesh, in_specs=in_specs, out_specs=out_specs, check_vma=False)
```

```python
import functools

import jax
import jax.numpy as jnp
from jax import lax
from jax.experimental import pallas as pl
from jax.experimental.pallas import tpu as pltpu
from jax.sharding import PartitionSpec as P


ITERS = 4
EPS = 1e-6
W = 384
HALF = W // 2
SC = 16
MSG = HALF + SC
SECTORS = 16
ENTRIES = float(SECTORS * W * W)
ORDER = {0: 0, 1: 1, 3: 2, 2: 3}
F32 = jnp.float32
BF16 = jnp.bfloat16
VM = pl.BlockSpec(memory_space=pltpu.VMEM)
SM = pl.BlockSpec(memory_space=pltpu.SMEM)
PARAMS = pltpu.CompilerParams(vmem_limit_bytes=16 * 1024 * 1024)


def kernel_call(body, out_shape, in_specs, scratch=(), aliases=None):
    call = pl.pallas_call(
        body,
        out_shape=jax.tree.map(lambda s: pltpu.VMEM(s.shape, s.dtype), out_shape),
        in_specs=in_specs,
        out_specs=jax.tree.map(lambda _: VM, out_shape),
        scratch_shapes=scratch,
        input_output_aliases=aliases or {},
        compiler_params=PARAMS,
    )

    def run(*operands):
        placed = [
            pltpu.with_memory_space_constraint(x, pltpu.VMEM) if spec is VM else x
            for x, spec in zip(operands, in_specs)
        ]
        return call(*placed)

    return run


def triple(values):
    tall = jnp.concatenate(
        [jnp.broadcast_to(v, (1, 128)) for v in values] + [jnp.zeros((SC - len(values), 128), F32)], axis=0
    )
    high = tall.astype(BF16)
    rest = tall - high.astype(F32)
    mid = rest.astype(BF16)
    low = (rest - mid.astype(F32)).astype(BF16)
    return jnp.concatenate([high, mid, low], axis=1)


def sums_of(tile):
    tall = tile[:, 0:128] + tile[:, 128:256] + tile[:, 256:384]
    return [tall[k : k + 1, 0:1] for k in range(8)]


def total(x):
    return jnp.sum(jnp.sum(x, axis=0, keepdims=True), axis=1, keepdims=True)


def piece(groups, r, stride):
    outer, at = r >> 2, ORDER[r & 3]
    own, one, three, two_low, two_high = groups
    if outer == 2:
        return (two_low, at * stride) if at < 2 else (two_high, (at - 2) * stride)
    return {0: own, 1: one, 3: three}[outer], at * stride


def sector_sums(core, groups, stride):
    tiles = []
    for r in range(SECTORS):
        ref, row = piece(groups, r, stride)
        tiles.append(ref[row + HALF : row + MSG, :].astype(F32))
    straight = core == 0
    tiles = {r: jnp.where(straight, tiles[r], tiles[(r >> 2) | ((r & 3) << 2)]) for r in range(SECTORS)}
    for bit in (1, 2, 4, 8):
        tiles = {r: t + tiles[r ^ bit] for r, t in tiles.items() if not r & bit}
    return sums_of(tiles[0])


def prep_kernel(core, start, precond, x_own, q_own, msg, xt, qt):
    c = core[0]
    xt[...] = jnp.transpose(start[...])
    qt[...] = 1.0 / jnp.transpose(precond[...])
    here, there = pl.multiple_of(c * HALF, HALF), pl.multiple_of((1 - c) * HALF, HALF)
    x_own[0:HALF, :] = xt[pl.ds(here, HALF), :]
    x_own[HALF:W, :] = xt[pl.ds(there, HALF), :]
    q_own[0:HALF, :] = qt[pl.ds(here, HALF), :]
    q_own[HALF:W, :] = qt[pl.ds(there, HALF), :]
    x = x_own[...]
    msg[0:HALF, :] = x[0:HALF].astype(BF16)
    msg[HALF:MSG, :] = triple([total(x * x)])
    msg[MSG : MSG + HALF, :] = q_own[0:HALF, :].astype(BF16)


def halves_kernel(core, right, here, there):
    straight = core[0] == 0

    def cut(j, carry):
        block = right[j]
        low, high = block[:, :HALF], block[:, HALF:]
        here[j] = jnp.where(straight, low, high)
        there[j] = jnp.where(straight, high, low)
        return carry

    lax.fori_loop(0, right.shape[0], cut, 0)


def contract(tables, ops, xs, acc):
    acc[...] = jnp.zeros_like(acc)
    for (pos, count), (left, right) in zip(tables, ops):

        def slot(j, carry):
            product = lax.dot_general(
                xs[pos[j]], left[j], (((1,), (1,)), ((), ())), preferred_element_type=F32
            ).astype(BF16)
            acc[...] += jnp.dot(right[j], product, preferred_element_type=F32)
            return carry

        lax.fori_loop(0, count[0], slot, 0)


def emit(c, acc, v_own, d_own, keep, send):
    here, there = pl.multiple_of(c * HALF, HALF), pl.multiple_of((1 - c) * HALF, HALF)
    mine, other = acc[pl.ds(here, HALF), :], acc[pl.ds(there, HALF), :]
    keep[...] = mine
    values = [total(x[0:HALF, :] * mine + x[HALF:W, :] * other) for x in (v_own, d_own) if x is not None]
    send[0:HALF, :] = other.astype(BF16)
    send[HALF:MSG, :] = triple(values)


def first_kernel(*refs):
    core, pos, count, pos2, count2 = refs[:5]
    groups = refs[5:10]
    x_own, left, right, left2, right2 = refs[10:15]
    state, v_own, v, q, xs, known, keep, send, acc = refs[15:]
    stride = MSG + HALF
    norm = sector_sums(core[0], groups, stride)[0] / ENTRIES
    scale = 1.0 / jnp.sqrt(norm + EPS)
    state[0:1, :] = jnp.broadcast_to(norm * scale * scale, (1, 128))
    state[1:8, :] = jnp.zeros((7, 128), F32)
    known[...] = jnp.zeros_like(known)
    v_own[...] = x_own[...] * scale
    for r in range(SECTORS):
        ref, row = piece(groups, r, stride)
        vector = ref[row : row + HALF, :].astype(F32) * scale
        v[r] = vector
        xs[r] = vector.astype(BF16)
        q[r] = ref[row + MSG : row + MSG + HALF, :]
    contract(((pos, count), (pos2, count2)), ((left, right), (left2, right2)), xs, acc)
    emit(core[0], acc, v_own, None, keep, send)


def step_scalars(state, sums):
    vz, dz, vd, dd, dw = [s / ENTRIES for s in sums[:5]]
    vv, vw = state[0:1, 0:1], state[1:2, 0:1]
    along = vd
    inverse = 1.0 / jnp.sqrt(dd - 2.0 * along * vd + along * along * vv + EPS)
    left = inverse * (vz - along * vw)
    right = inverse * (dw - along * vw)
    corner = inverse * inverse * (dz - along * (vz + dw) + along * along * vw)
    coupling = 0.5 * (left + right)
    half_gap = 0.5 * (vw - corner)
    ritz = 0.5 * (vw + corner) - jnp.sqrt(half_gap * half_gap + coupling * coupling)
    weight_old = corner - ritz
    alpha = weight_old + coupling * inverse * along
    beta = -coupling * inverse
    norm = alpha * alpha * vv + 2.0 * alpha * beta * vd + beta * beta * dd
    factor = 1.0 / jnp.sqrt(norm + EPS)
    alpha, beta = alpha * factor, beta * factor
    new_vv = norm * factor * factor
    theta = alpha * alpha * vw + alpha * beta * (vz + dw) + beta * beta * dz
    return alpha, beta, new_vv, theta, ritz


def step_kernel(iteration, *refs):
    core, pos, count, pos2, count2 = refs[:5]
    groups = refs[5:10]
    other_z, old_state, old_v_own, old_w_own, old_d_own, q_own = refs[10:16]
    old_v, old_w, q, old_xs, left, right, left2, right2 = refs[16:24]
    state, v_own, w_own, d_own, v, w, xs, known, keep, send, acc = refs[24:]
    first = iteration == 0
    sums = sector_sums(core[0], groups, MSG)
    own_z = jnp.concatenate([groups[0][0:HALF, :], other_z[0:HALF, :]], axis=0).astype(F32)
    state[...] = old_state[...]
    if first:
        theta = sums[0] / ENTRIES
        v_o, w_o = old_v_own[...], own_z
    else:
        alpha, beta, new_vv, theta, ritz = step_scalars(old_state, sums)
        state[0:1, :] = jnp.broadcast_to(new_vv, (1, 128))
        state[3 + iteration : 4 + iteration, :] = jnp.broadcast_to(ritz, (1, 128))
        v_o = alpha * old_v_own[...] + beta * old_d_own[...]
        w_o = alpha * old_w_own[...] + beta * own_z
    state[1:2, :] = jnp.broadcast_to(theta, (1, 128))
    d_o = (w_o - theta * v_o) * q_own[...]
    v_own[...] = v_o
    w_own[...] = w_o
    d_own[...] = d_o
    parts = [total(v_o * d_o), total(d_o * d_o), total(d_o * w_o)]
    known[...] = jnp.concatenate(
        [jnp.broadcast_to(x, (1, 128)) for x in parts] + [jnp.zeros((5, 128), F32)], axis=0
    )
    for r in range(SECTORS):
        ref, row = piece(groups, r, MSG)
        z = ref[row : row + HALF, :].astype(F32)
        if first:
            vector, image = old_v[r], z
        else:
            vector = alpha * old_v[r] + beta * old_xs[r].astype(F32)
            image = alpha * old_w[r] + beta * z
            v[r] = vector
        w[r] = image
        xs[r] = ((image - theta * vector) * q[r].astype(F32)).astype(BF16)
    contract(((pos, count), (pos2, count2)), ((left, right), (left2, right2)), xs, acc)
    emit(core[0], acc, v_own, d_own, keep, send)


def pair_sums(chip, mine, came):
    both = sums_of(mine.astype(F32) + came.astype(F32))
    return triple([jnp.where(chip == k // 2, both[k % 2], 0.0) for k in range(8)])


def pair_kernel(chip, keep, send, came, out):
    out[0:HALF, :] = (keep[...] + came[0:HALF, :].astype(F32)).astype(BF16)
    out[HALF:MSG, :] = pair_sums(chip[0], send[HALF:MSG, :], came[HALF:MSG, :])


def two_kernel(own, came, out):
    out[...] = (own[...].astype(F32) + came[...].astype(F32)).astype(BF16)


def chip_sums(tile, known):
    at = sums_of(tile)
    vz, dz = (at[k] + at[k + 2] + at[k + 4] + at[k + 6] for k in (0, 1))
    return [vz, dz] + [known[k : k + 1, 0:1] for k in range(3)]


def four_kernel(own, came, known, out):
    z = own[...].astype(F32) + came[...].astype(F32)
    out[0:HALF, :] = z[0:HALF].astype(BF16)
    out[HALF:MSG, :] = triple(chip_sums(z[HALF:MSG], known))


def tail_pair_kernel(chip, send, came, out):
    out[...] = pair_sums(chip[0], send[HALF:MSG, :], came[...])


def tail_four_kernel(one, two, three, own, known, out):
    tile = (own[...].astype(F32) + one[...].astype(F32)) + (two[...].astype(F32) + three[...].astype(F32))
    out[...] = triple(chip_sums(tile, known))


def row_kernel(own, one, two, three, out):
    tile = (own[...].astype(F32) + one[...].astype(F32)) + (two[...].astype(F32) + three[...].astype(F32))
    out[...] = triple(sums_of(tile))


def last_kernel(core, one, two, three, own, old_state, v_own, d_own, vector, ritz, turned):
    c = core[0]
    tiles = (own[...].astype(F32) + one[...].astype(F32)) + (two[...].astype(F32) + three[...].astype(F32))
    alpha, beta, _, _, lowest = step_scalars(old_state, sums_of(tiles))
    ritz[...] = old_state[...]
    ritz[3 + ITERS : 4 + ITERS, :] = jnp.broadcast_to(lowest, (1, 128))
    here, there = pl.multiple_of(c * HALF, HALF), pl.multiple_of((1 - c) * HALF, HALF)
    turned[pl.ds(here, HALF), :] = alpha * v_own[0:HALF, :] + beta * d_own[0:HALF, :]
    turned[pl.ds(there, HALF), :] = alpha * v_own[HALF:W, :] + beta * d_own[HALF:W, :]
    vector[...] = jnp.transpose(turned[...])


def shape(*dims, dtype=F32):
    return jax.ShapeDtypeStruct(dims, dtype)


def routes(*masks):
    both = [masks[0], masks[-1]]

    def run(x):
        term, sector = lax.axis_size("term"), lax.axis_size("sector")
        perm = []
        for t in range(term):
            for s in range(sector):
                dt, ds = both[t % 2]
                perm.append((t * sector + s, (t ^ dt) * sector + (s ^ ds)))
        return lax.ppermute(x, ("term", "sector"), perm)

    return run


PAIR = routes((1, 0))
CHIP = {k: routes((2 * k, 0)) for k in (1, 2, 3)}
CHIP_A, CHIP_B = routes((2, 0), (6, 0)), routes((6, 0), (2, 0))
INNER = {k: routes((0, k), (0, 4 * k)) for k in (1, 2, 3)}
OUTER = {k: routes((0, 4 * k), (0, k)) for k in (1, 2, 3)}


def gather_blocks(msg):
    own = jnp.concatenate([msg, INNER[1](msg), INNER[3](msg), INNER[2](msg)], axis=0)
    one, three = OUTER[1](own), OUTER[3](own)
    cut = 2 * msg.shape[0]
    return own, one, three, OUTER[1](three[:cut]), OUTER[3](one[cut:])


def shards(start_vector, precond, op_left, op_right, slot_source, slot_count):
    left, right = op_left[0, 0], op_right[0, 0]
    slots = left.shape[0]
    me = lax.axis_index("sector")
    term = lax.axis_index("term")
    c, x = term % 2, term // 2
    core, chip = c[None].astype(jnp.int32), x[None].astype(jnp.int32)

    table = jnp.concatenate([slot_source[0, 0] ^ me, slot_count[0]])
    table2 = PAIR(table)

    def places(sources):
        return jnp.where(c == 0, sources, (sources >> 2) | ((sources & 3) << 2))

    tables = (places(table[:slots]), table[slots:], places(table2[:slots]), table2[slots:])
    half = functools.partial(shape, slots, W, HALF, dtype=BF16)
    right_here, right_there = kernel_call(halves_kernel, [half(), half()], [SM, VM])(core, right)
    ops = (left, right_here, PAIR(left), PAIR(right_there))

    x_own, q_own, msg = kernel_call(
        prep_kernel,
        [shape(W, W), shape(W, W), shape(MSG + HALF, W, dtype=BF16)],
        [SM, VM, VM],
        [pltpu.VMEM((W, W), F32)] * 2,
    )(core, start_vector[0], precond[0])
    groups = gather_blocks(msg)

    field = functools.partial(shape, SECTORS, HALF, W)
    outs = [shape(8, 128), shape(HALF, W), shape(MSG, W, dtype=BF16)]
    acc = [pltpu.VMEM((W, W), F32)]
    state, v_own, v, q, xs, known, keep, send = kernel_call(
        first_kernel,
        [shape(8, 128), shape(W, W), field(), field(dtype=BF16), field(dtype=BF16)] + outs,
        [SM] * 5 + [VM] * 10,
        acc,
    )(core, *tables, *groups, x_own, *ops)
    w_own, d_own = v_own, v_own
    w = v
    message = shape(MSG, W, dtype=BF16)

    for iteration in range(ITERS):
        both = kernel_call(pair_kernel, message, [SM] + [VM] * 3)(chip, keep, send, PAIR(send))
        two = kernel_call(two_kernel, message, [VM] * 2)(both, CHIP_A(both))
        msg = kernel_call(four_kernel, message, [VM] * 3)(two, CHIP_B(two), known)
        other_z = PAIR(msg)
        groups = gather_blocks(msg)
        state, v_own, w_own, d_own, v, w, xs, known, keep, send = kernel_call(
            functools.partial(step_kernel, iteration),
            [shape(8, 128), shape(W, W), shape(W, W), shape(W, W), field(), field(), field(dtype=BF16)] + outs,
            [SM] * 5 + [VM] * 19,
            acc,
            {11: 0, 16: 4, 19: 6} if iteration == 0 else {11: 0, 12: 1, 13: 2, 14: 3, 16: 4, 17: 5, 19: 6},
        )(core, *tables, *groups, other_z, state, v_own, w_own, d_own, q_own, v, w, q, xs, *ops)

    small = shape(SC, W, dtype=BF16)
    tile = kernel_call(tail_pair_kernel, small, [SM] + [VM] * 2)(chip, send, PAIR(send[HALF:]))
    tile = kernel_call(tail_four_kernel, small, [VM] * 5)(CHIP[1](tile), CHIP[2](tile), CHIP[3](tile), tile, known)
    along_y = [tile] + [routes((0, k))(tile) for k in (1, 2, 3)]
    tile = kernel_call(row_kernel, small, [VM] * 4)(*along_y)
    vector, ritz = kernel_call(
        last_kernel,
        [shape(W, W), shape(8, 128)],
        [SM] + [VM] * 7,
        [pltpu.VMEM((W, W), F32)],
    )(core, *[routes((0, 4 * k))(tile) for k in (1, 2, 3)], tile, state, v_own, d_own)
    return vector[None], ritz[8 - ITERS :, 0]


def solution(mesh):
    in_specs = (
        P("sector", None, None),
        P("sector", None, None),
        P("term", "sector", None, None, None),
        P("term", "sector", None, None, None),
        P("term", "sector", None),
        P("term", "sector"),
    )
    out_specs = (P("sector", None, None), P())
    return jax.shard_map(shards, mesh=mesh, in_specs=in_specs, out_specs=out_specs, check_vma=False)
```

```python
import functools

import jax
import jax.numpy as jnp
from jax import lax
from jax.experimental import pallas as pl
from jax.experimental.pallas import tpu as pltpu
from jax.sharding import PartitionSpec as P


ITERS = 4
EPS = 1e-6
W = 384
HALF = W // 2
SC = 16
MSG = HALF + SC
SECTORS = 16
GROUP = 4
ROWS = 32
ENTRIES = float(SECTORS * W * W)
F32 = jnp.float32
BF16 = jnp.bfloat16
VM = pl.BlockSpec(memory_space=pltpu.VMEM)
SM = pl.BlockSpec(memory_space=pltpu.SMEM)
ANY = pl.BlockSpec(memory_space=pl.ANY)
PARAMS = pltpu.CompilerParams(vmem_limit_bytes=6 * 1024 * 1024)


def kernel_call(body, out_shape, in_specs, scratch=(), aliases=None):
    call = pl.pallas_call(
        body,
        out_shape=jax.tree.map(lambda s: pltpu.VMEM(s.shape, s.dtype), out_shape),
        in_specs=in_specs,
        out_specs=jax.tree.map(lambda _: VM, out_shape),
        scratch_shapes=scratch,
        input_output_aliases=aliases or {},
        compiler_params=PARAMS,
    )

    def run(*operands):
        placed = [
            pltpu.with_memory_space_constraint(x, pltpu.VMEM) if spec is VM else x
            for x, spec in zip(operands, in_specs)
        ]
        return call(*placed)

    return run


def triple(values):
    tall = jnp.concatenate(
        [jnp.broadcast_to(v, (1, 128)) for v in values] + [jnp.zeros((SC - len(values), 128), F32)], axis=0
    )
    high = tall.astype(BF16)
    rest = tall - high.astype(F32)
    mid = rest.astype(BF16)
    low = (rest - mid.astype(F32)).astype(BF16)
    return jnp.concatenate([high, mid, low], axis=1)


def sums_of(tile):
    tall = tile[:, 0:128] + tile[:, 128:256] + tile[:, 256:384]
    return [tall[k : k + 1, 0:1] for k in range(8)]


def total(x):
    return jnp.sum(jnp.sum(x, axis=0, keepdims=True), axis=1, keepdims=True)


def places_of(index):
    outer, high = (0, 0, 1, 1, 3, 3, 2, 2)[index], index % 2
    return (4 * outer + 3, -1) if high else (4 * outer, 1)


def sector_sums(core, groups):
    found = {}
    for index, ref in enumerate(groups):
        base, step = places_of(index)
        for k in (0, 1):
            found[base + step * k] = ref[k * MSG + HALF : (k + 1) * MSG, :].astype(F32)
    straight = core == 0
    tiles = {r: jnp.where(straight, found[r], found[(r >> 2) | ((r & 3) << 2)]) for r in range(SECTORS)}
    for bit in (1, 2, 4, 8):
        tiles = {r: t + tiles[r ^ bit] for r, t in tiles.items() if not r & bit}
    return sums_of(tiles[0])


def each_chunk(groups, body):
    for index in range(len(groups)):
        base, step = places_of(index)
        for k in (0, 1):

            def chunk(i, carry, index=index, r=base + step * k, k=k):
                body(index, r, k, pl.multiple_of(i * ROWS, ROWS))
                return carry

            lax.fori_loop(0, HALF // ROWS, chunk, 0, unroll=2)


def prep_kernel(core, start, precond, x_own, q_own, msg, q_msg, xt, qt):
    c = core[0]
    xt[...] = jnp.transpose(start[...])
    qt[...] = 1.0 / jnp.transpose(precond[...])
    here, there = pl.multiple_of(c * HALF, HALF), pl.multiple_of((1 - c) * HALF, HALF)
    x_own[0:HALF, :] = xt[pl.ds(here, HALF), :]
    x_own[HALF:W, :] = xt[pl.ds(there, HALF), :]
    q_own[0:HALF, :] = qt[pl.ds(here, HALF), :]
    q_own[HALF:W, :] = qt[pl.ds(there, HALF), :]
    x = x_own[...]
    msg[0:HALF, :] = x[0:HALF].astype(BF16)
    msg[HALF:MSG, :] = triple([total(x * x)])
    q_msg[...] = q_own[0:HALF, :].astype(BF16)


def halves_kernel(core, right, here, there):
    straight = core[0] == 0

    def cut(j, carry):
        one, two = right[2 * j], right[2 * j + 1]
        low = jnp.concatenate([one[:, :HALF], two[:, :HALF]], axis=1)
        high = jnp.concatenate([one[:, HALF:], two[:, HALF:]], axis=1)
        at = pl.ds(pl.multiple_of(j * W, W), W)
        here[:, at] = jnp.where(straight, low, high)
        there[:, at] = jnp.where(straight, high, low)
        return carry

    lax.fori_loop(0, right.shape[0] // 2, cut, 0)


def settle_kernel(left, right, left_out, right_out, sems):
    copies = [
        pltpu.make_async_copy(left, left_out, sems.at[0]),
        pltpu.make_async_copy(right, right_out, sems.at[1]),
    ]
    for copy in copies:
        copy.start()
    for copy in copies:
        copy.wait()


def contract(table, ops, xs, acc):
    acc[...] = jnp.zeros_like(acc)
    for index, (left, right) in enumerate(ops):
        slots = left.shape[0]
        first = 1 + index * (slots + 1)
        live = table[first + slots]

        def group(j, carry):
            products = []
            for k in range(GROUP):
                slot = j * GROUP + k
                product = lax.dot_general(
                    xs[table[first + slot]], left[slot], (((1,), (1,)), ((), ())), preferred_element_type=F32
                )
                if k:
                    product = jnp.where(slot < live, product, 0.0)
                products.append(product.astype(BF16))
            at = pl.ds(pl.multiple_of(j * (GROUP * HALF), GROUP * HALF), GROUP * HALF)
            acc[...] += jnp.dot(right[:, at], jnp.concatenate(products, axis=0), preferred_element_type=F32)
            return carry

        lax.fori_loop(0, (live + GROUP - 1) // GROUP, group, 0)


def emit(c, acc, v_own, d_own, keep, send):
    here, there = c * HALF, (1 - c) * HALF
    fields = [x for x in (v_own, d_own) if x is not None]
    parts = [jnp.zeros((ROWS, W), F32) for _ in fields]
    for i in range(0, HALF, ROWS):
        mine = acc[pl.ds(pl.multiple_of(here + i, ROWS), ROWS), :]
        other = acc[pl.ds(pl.multiple_of(there + i, ROWS), ROWS), :]
        parts = [
            p + x[i : i + ROWS, :] * mine + x[HALF + i : HALF + i + ROWS, :] * other for p, x in zip(parts, fields)
        ]
        if keep is not None:
            keep[i : i + ROWS, :] = mine
            send[i : i + ROWS, :] = other.astype(BF16)
    tile = triple([total(p) for p in parts])
    if keep is None:
        send[...] = tile
    else:
        send[HALF:MSG, :] = tile


def first_kernel(*refs):
    table = refs[0]
    groups = refs[1:9]
    x_own, left, right, left2, right2 = refs[9:14]
    state, v_own, v, xs, known, keep, send, acc = refs[14:]
    norm = sector_sums(table[0], groups)[0] / ENTRIES
    scale = 1.0 / jnp.sqrt(norm + EPS)
    state[0:1, :] = jnp.broadcast_to(norm * scale * scale, (1, 128))
    state[1:8, :] = jnp.zeros((7, 128), F32)
    known[...] = jnp.zeros_like(known)
    for i in range(0, W, ROWS):
        v_own[i : i + ROWS, :] = x_own[i : i + ROWS, :] * scale

    def chunk(index, r, k, row):
        vector = groups[index][pl.ds(k * MSG + row, ROWS), :].astype(F32) * scale
        at = pl.ds(row, ROWS)
        v[r, at, :] = vector
        xs[r, at, :] = vector.astype(BF16)

    each_chunk(groups, chunk)
    contract(table, ((left, right), (left2, right2)), xs, acc)
    emit(table[0], acc, v_own, None, keep, send)


def step_scalars(state, sums):
    vz, dz, vd, dd, dw = [s / ENTRIES for s in sums[:5]]
    vv, vw = state[0:1, 0:1], state[1:2, 0:1]
    along = vd
    inverse = 1.0 / jnp.sqrt(dd - 2.0 * along * vd + along * along * vv + EPS)
    left = inverse * (vz - along * vw)
    right = inverse * (dw - along * vw)
    corner = inverse * inverse * (dz - along * (vz + dw) + along * along * vw)
    coupling = 0.5 * (left + right)
    half_gap = 0.5 * (vw - corner)
    ritz = 0.5 * (vw + corner) - jnp.sqrt(half_gap * half_gap + coupling * coupling)
    weight_old = corner - ritz
    alpha = weight_old + coupling * inverse * along
    beta = -coupling * inverse
    norm = alpha * alpha * vv + 2.0 * alpha * beta * vd + beta * beta * dd
    factor = 1.0 / jnp.sqrt(norm + EPS)
    alpha, beta = alpha * factor, beta * factor
    new_vv = norm * factor * factor
    theta = alpha * alpha * vw + alpha * beta * (vz + dw) + beta * beta * dz
    return alpha, beta, new_vv, theta, ritz


def step_kernel(first, *refs):
    table = refs[0]
    groups, q_groups = refs[1:9], refs[9:17]
    other_z, q_own, left, right, left2, right2, old_state, old_v_own, old_v, old_xs = refs[17:27]
    old_w_own, old_d_own, old_w = (None, None, None) if first else refs[27:30]
    state, v_own, w_own, d_own, v, w, xs, known, *sent, acc = refs[27 if first else 30 :]
    sums = sector_sums(table[0], groups)
    if first:
        theta = sums[0] / ENTRIES
        state[...] = old_state[...]
    else:
        alpha, beta, new_vv, theta, ritz = step_scalars(old_state, sums)
        state[0:1, :] = jnp.broadcast_to(new_vv, (1, 128))
        state[2:7, :] = old_state[3:8, :]
        state[7:8, :] = jnp.broadcast_to(ritz, (1, 128))
    state[1:2, :] = jnp.broadcast_to(theta, (1, 128))

    def own_chunk(half, ref, i, parts):
        row = pl.multiple_of(i * ROWS, ROWS)
        at = pl.ds(pl.multiple_of(half + row, ROWS), ROWS)
        z = ref[pl.ds(row, ROWS), :].astype(F32)
        if first:
            vector, image = old_v_own[at, :], z
        else:
            vector = alpha * old_v_own[at, :] + beta * old_d_own[at, :]
            image = alpha * old_w_own[at, :] + beta * z
        direct = (image - theta * vector) * q_own[at, :]
        v_own[at, :] = vector
        w_own[at, :] = image
        d_own[at, :] = direct
        return tuple(p + direct * x for p, x in zip(parts, (vector, direct, image)))

    parts = tuple(jnp.zeros((ROWS, W), F32) for _ in range(3))
    for half, ref in ((0, groups[0]), (HALF, other_z)):
        parts = lax.fori_loop(0, HALF // ROWS, functools.partial(own_chunk, half, ref), parts)
    known[...] = jnp.concatenate(
        [jnp.broadcast_to(total(p), (1, 128)) for p in parts] + [jnp.zeros((5, 128), F32)], axis=0
    )

    def chunk(index, r, k, row):
        at = pl.ds(row, ROWS)
        z = groups[index][pl.ds(k * MSG + row, ROWS), :].astype(F32)
        q = q_groups[index][pl.ds(k * HALF + row, ROWS), :].astype(F32)
        if first:
            vector, image = old_v[r, at, :], z
        else:
            vector = alpha * old_v[r, at, :] + beta * old_xs[r, at, :].astype(F32)
            image = alpha * old_w[r, at, :] + beta * z
            v[r, at, :] = vector
        w[r, at, :] = image
        xs[r, at, :] = ((image - theta * vector) * q).astype(BF16)

    each_chunk(groups, chunk)
    contract(table, ((left, right), (left2, right2)), xs, acc)
    emit(table[0], acc, v_own, d_own, *([None] * (2 - len(sent)) + sent))


def pair_sums(chip, mine, came):
    both = sums_of(mine.astype(F32) + came.astype(F32))
    return triple([jnp.where(chip == k // 2, both[k % 2], 0.0) for k in range(8)])


def pair_kernel(chip, keep, send, came, out):
    out[0:HALF, :] = (keep[...] + came[0:HALF, :].astype(F32)).astype(BF16)
    out[HALF:MSG, :] = pair_sums(chip[0], send[HALF:MSG, :], came[HALF:MSG, :])


def two_kernel(own, came, out):
    out[...] = (own[...].astype(F32) + came[...].astype(F32)).astype(BF16)


def chip_sums(tile, known):
    at = sums_of(tile)
    vz, dz = (at[k] + at[k + 2] + at[k + 4] + at[k + 6] for k in (0, 1))
    return [vz, dz] + [known[k : k + 1, 0:1] for k in range(3)]


def four_kernel(own, came, known, out):
    z = own[...].astype(F32) + came[...].astype(F32)
    out[0:HALF, :] = z[0:HALF].astype(BF16)
    out[HALF:MSG, :] = triple(chip_sums(z[HALF:MSG], known))


def tail_pair_kernel(chip, send, came, out):
    out[...] = pair_sums(chip[0], send[...], came[...])


def tail_four_kernel(one, two, three, own, known, out):
    tile = (own[...].astype(F32) + one[...].astype(F32)) + (two[...].astype(F32) + three[...].astype(F32))
    out[...] = triple(chip_sums(tile, known))


def row_kernel(own, one, two, three, out):
    tile = (own[...].astype(F32) + one[...].astype(F32)) + (two[...].astype(F32) + three[...].astype(F32))
    out[...] = triple(sums_of(tile))


def last_kernel(core, one, two, three, own, old_state, v_own, d_own, vector, ritz, turned):
    c = core[0]
    tiles = (own[...].astype(F32) + one[...].astype(F32)) + (two[...].astype(F32) + three[...].astype(F32))
    alpha, beta, _, _, lowest = step_scalars(old_state, sums_of(tiles))
    ritz[0:7, :] = old_state[1:8, :]
    ritz[7:8, :] = jnp.broadcast_to(lowest, (1, 128))
    here, there = pl.multiple_of(c * HALF, HALF), pl.multiple_of((1 - c) * HALF, HALF)
    turned[pl.ds(here, HALF), :] = alpha * v_own[0:HALF, :] + beta * d_own[0:HALF, :]
    turned[pl.ds(there, HALF), :] = alpha * v_own[HALF:W, :] + beta * d_own[HALF:W, :]
    vector[...] = jnp.transpose(turned[...])


def shape(*dims, dtype=F32):
    return jax.ShapeDtypeStruct(dims, dtype)


def routes(*masks):
    both = [masks[0], masks[-1]]

    def run(x):
        term, sector = lax.axis_size("term"), lax.axis_size("sector")
        perm = []
        for t in range(term):
            for s in range(sector):
                dt, ds = both[t % 2]
                perm.append((t * sector + s, (t ^ dt) * sector + (s ^ ds)))
        return lax.ppermute(x, ("term", "sector"), perm)

    return run


PAIR = routes((1, 0))
CHIP = {k: routes((2 * k, 0)) for k in (1, 2, 3)}
CHIP_A, CHIP_B = routes((2, 0), (6, 0)), routes((6, 0), (2, 0))
INNER = {k: routes((0, k), (0, 4 * k)) for k in (1, 2, 3)}
OUTER = {k: routes((0, 4 * k), (0, k)) for k in (1, 2, 3)}


def gather_blocks(msg):
    low = jnp.concatenate([msg, INNER[1](msg)], axis=0)
    high = jnp.concatenate([INNER[3](msg), INNER[2](msg)], axis=0)
    one_low, three_low = OUTER[1](low), OUTER[3](low)
    one_high, three_high = OUTER[1](high), OUTER[3](high)
    return low, high, one_low, one_high, three_low, three_high, OUTER[1](three_low), OUTER[3](one_high)


def shards(start_vector, precond, op_left, op_right, slot_source, slot_count):
    left, right = op_left[0, 0], op_right[0, 0]
    slots = left.shape[0]
    me = lax.axis_index("sector")
    term = lax.axis_index("term")
    c, x = term % 2, term // 2
    core, chip = c[None].astype(jnp.int32), x[None].astype(jnp.int32)

    sources = slot_source[0, 0] ^ me
    mine = jnp.concatenate([sources, slot_count[0]])
    theirs = PAIR(mine)
    table = jnp.concatenate([mine, theirs])
    is_source = jnp.arange(table.shape[0]) % (slots + 1) < slots
    turned = (table >> 2) | ((table & 3) << 2)
    table = jnp.concatenate([core, jnp.where((c == 1) & is_source, turned, table)])
    half = functools.partial(shape, W, slots * HALF, dtype=BF16)
    right_here, right_there = kernel_call(halves_kernel, [half(), half()], [SM, VM])(core, right)
    left2, right2 = kernel_call(
        settle_kernel,
        [shape(slots, W, W, dtype=BF16), half()],
        [ANY, ANY],
        [pltpu.SemaphoreType.DMA((2,))],
    )(PAIR(left), PAIR(right_there))
    ops = (left, right_here, left2, right2)

    x_own, q_own, msg, q_msg = kernel_call(
        prep_kernel,
        [shape(W, W), shape(W, W), shape(MSG, W, dtype=BF16), shape(HALF, W, dtype=BF16)],
        [SM, VM, VM],
        [pltpu.VMEM((W, W), F32)] * 2,
    )(core, start_vector[0], precond[0])
    groups = gather_blocks(msg)
    q_groups = gather_blocks(q_msg)

    field = functools.partial(shape, SECTORS, HALF, W)
    message, small = shape(MSG, W, dtype=BF16), shape(SC, W, dtype=BF16)
    outs = [shape(8, 128), shape(HALF, W), message]
    acc = [pltpu.VMEM((W, W), F32)]
    state, v_own, v, xs, known, *sent = kernel_call(
        first_kernel,
        [shape(8, 128), shape(W, W), field(), field(dtype=BF16)] + outs,
        [SM] + [VM] * 13,
        acc,
    )(table, *groups, x_own, *ops)
    older = ()

    for iteration in range(ITERS):
        both = kernel_call(pair_kernel, message, [SM] + [VM] * 3)(chip, *sent, PAIR(sent[1]))
        two = kernel_call(two_kernel, message, [VM] * 2)(both, CHIP_A(both))
        msg = kernel_call(four_kernel, message, [VM] * 3)(two, CHIP_B(two), known)
        other_z = PAIR(msg)
        groups = gather_blocks(msg)
        if iteration + 1 == ITERS:
            outs = [shape(8, 128), small]
        aliases = {23: 0, 24: 1, 25: 4, 26: 6}
        state, v_own, w_own, d_own, v, w, xs, known, *sent = kernel_call(
            functools.partial(step_kernel, iteration == 0),
            [shape(8, 128), shape(W, W), shape(W, W), shape(W, W), field(), field(), field(dtype=BF16)] + outs,
            [SM] + [VM] * (26 + len(older)),
            acc,
            aliases if iteration == 0 else aliases | {27: 2, 28: 3, 29: 5},
        )(table, *groups, *q_groups, other_z, q_own, *ops, state, v_own, v, xs, *older)
        older = (w_own, d_own, w)

    tile = kernel_call(tail_pair_kernel, small, [SM] + [VM] * 2)(chip, *sent, PAIR(*sent))
    tile = kernel_call(tail_four_kernel, small, [VM] * 5)(CHIP[1](tile), CHIP[2](tile), CHIP[3](tile), tile, known)
    along_y = [tile] + [routes((0, k))(tile) for k in (1, 2, 3)]
    tile = kernel_call(row_kernel, small, [VM] * 4)(*along_y)
    vector, ritz = kernel_call(
        last_kernel,
        [shape(W, W), shape(8, 128)],
        [SM] + [VM] * 7,
        [pltpu.VMEM((W, W), F32)],
    )(core, *[routes((0, 4 * k))(tile) for k in (1, 2, 3)], tile, state, v_own, d_own)
    return vector[None], ritz[8 - ITERS :, 0]


def solution(mesh):
    in_specs = (
        P("sector", None, None),
        P("sector", None, None),
        P("term", "sector", None, None, None),
        P("term", "sector", None, None, None),
        P("term", "sector", None),
        P("term", "sector"),
    )
    out_specs = (P("sector", None, None), P())
    return jax.shard_map(shards, mesh=mesh, in_specs=in_specs, out_specs=out_specs, check_vma=False)
```

```python
import functools

import jax
import jax.numpy as jnp
from jax import lax
from jax.experimental import pallas as pl
from jax.experimental.pallas import tpu as pltpu
from jax.sharding import PartitionSpec as P


ITERS = 4
EPS = 1e-6
W = 384
HALF = W // 2
SC = 16
MSG = HALF + SC
SECTORS = 16
GROUP = 4
ROWS = 32
ENTRIES = float(SECTORS * W * W)
F32 = jnp.float32
BF16 = jnp.bfloat16
VM = pl.BlockSpec(memory_space=pltpu.VMEM)
SM = pl.BlockSpec(memory_space=pltpu.SMEM)
ANY = pl.BlockSpec(memory_space=pl.ANY)
PARAMS = pltpu.CompilerParams(vmem_limit_bytes=6 * 1024 * 1024)


def kernel_call(body, out_shape, in_specs, scratch=(), aliases=None):
    call = pl.pallas_call(
        body,
        out_shape=jax.tree.map(lambda s: pltpu.VMEM(s.shape, s.dtype), out_shape),
        in_specs=in_specs,
        out_specs=jax.tree.map(lambda _: VM, out_shape),
        scratch_shapes=scratch,
        input_output_aliases=aliases or {},
        compiler_params=PARAMS,
    )

    def run(*operands):
        placed = [
            pltpu.with_memory_space_constraint(x, pltpu.VMEM) if spec is VM else x
            for x, spec in zip(operands, in_specs)
        ]
        return call(*placed)

    return run


def triple(values):
    tall = jnp.concatenate(
        [jnp.broadcast_to(v, (1, 128)) for v in values] + [jnp.zeros((SC - len(values), 128), F32)], axis=0
    )
    high = tall.astype(BF16)
    rest = tall - high.astype(F32)
    mid = rest.astype(BF16)
    low = (rest - mid.astype(F32)).astype(BF16)
    return jnp.concatenate([high, mid, low], axis=1)


def sums_of(tile):
    tall = tile[:, 0:128] + tile[:, 128:256] + tile[:, 256:384]
    return [tall[k : k + 1, 0:1] for k in range(8)]


def total(x):
    return jnp.sum(jnp.sum(x, axis=0, keepdims=True), axis=1, keepdims=True)


def places_of(index):
    outer, high = (0, 0, 1, 1, 3, 3, 2, 2)[index], index % 2
    return (4 * outer + 3, -1) if high else (4 * outer, 1)


def sector_sums(core, groups):
    found = {}
    for index, ref in enumerate(groups):
        base, step = places_of(index)
        for k in (0, 1):
            found[base + step * k] = ref[k * MSG + HALF : (k + 1) * MSG, :].astype(F32)
    straight = core == 1
    tiles = {r: jnp.where(straight, found[r], found[(r >> 2) | ((r & 3) << 2)]) for r in range(SECTORS)}
    for bit in (1, 2, 4, 8):
        tiles = {r: t + tiles[r ^ bit] for r, t in tiles.items() if not r & bit}
    return sums_of(tiles[0])


def each_chunk(groups, body):
    for index in range(len(groups)):
        base, step = places_of(index)
        for k in (0, 1):

            def chunk(i, carry, index=index, r=base + step * k, k=k):
                body(index, r, k, pl.multiple_of(i * ROWS, ROWS))
                return carry

            lax.fori_loop(0, HALF // ROWS, chunk, 0, unroll=True)


def prep_kernel(core, start, precond, x_own, q_own, msg, q_msg, xt, qt):
    c = core[0]
    xt[...] = jnp.transpose(start[...])
    qt[...] = 1.0 / jnp.transpose(precond[...])
    here, there = pl.multiple_of(c * HALF, HALF), pl.multiple_of((1 - c) * HALF, HALF)
    x_own[0:HALF, :] = xt[pl.ds(here, HALF), :]
    x_own[HALF:W, :] = xt[pl.ds(there, HALF), :]
    q_own[0:HALF, :] = qt[pl.ds(here, HALF), :]
    q_own[HALF:W, :] = qt[pl.ds(there, HALF), :]
    x = x_own[...]
    msg[0:HALF, :] = x[0:HALF].astype(BF16)
    msg[HALF:MSG, :] = triple([total(x * x)])
    q_msg[...] = q_own[0:HALF, :].astype(BF16)


def halves_kernel(core, right, here, there):
    straight = core[0] == 0

    def cut(j, carry):
        one, two = right[2 * j], right[2 * j + 1]
        low = jnp.concatenate([one[:, :HALF], two[:, :HALF]], axis=1)
        high = jnp.concatenate([one[:, HALF:], two[:, HALF:]], axis=1)
        at = pl.ds(pl.multiple_of(j * W, W), W)
        here[:, at] = jnp.where(straight, low, high)
        there[:, at] = jnp.where(straight, high, low)
        return carry

    lax.fori_loop(0, right.shape[0] // 2, cut, 0)


def settle_kernel(left, right, left_out, right_out, sems):
    copies = [
        pltpu.make_async_copy(left, left_out, sems.at[0]),
        pltpu.make_async_copy(right, right_out, sems.at[1]),
    ]
    for copy in copies:
        copy.start()
    for copy in copies:
        copy.wait()


def contract(table, ops, xs, acc):
    acc[...] = jnp.zeros_like(acc)
    for index, (left, right) in enumerate(ops):
        slots = left.shape[0]
        first = 1 + index * (slots + 1)
        live = table[first + slots]

        def group(j, carry):
            products = []
            for k in range(GROUP):
                slot = j * GROUP + k
                product = lax.dot_general(
                    xs[table[first + slot]], left[slot], (((1,), (1,)), ((), ())), preferred_element_type=F32
                )
                if k:
                    product = jnp.where(slot < live, product, 0.0)
                products.append(product.astype(BF16))
            at = pl.ds(pl.multiple_of(j * (GROUP * HALF), GROUP * HALF), GROUP * HALF)
            acc[...] += jnp.dot(right[:, at], jnp.concatenate(products, axis=0), preferred_element_type=F32)
            return carry

        lax.fori_loop(0, (live + GROUP - 1) // GROUP, group, 0)


def emit(c, acc, v_own, d_own, known, keep, send):
    here, there = c * HALF, (1 - c) * HALF
    fields = [x for x in (v_own, d_own) if x is not None]
    parts = [jnp.zeros((ROWS, W), F32) for _ in fields]
    for i in range(0, HALF, ROWS):
        mine = acc[pl.ds(pl.multiple_of(here + i, ROWS), ROWS), :]
        other = acc[pl.ds(pl.multiple_of(there + i, ROWS), ROWS), :]
        parts = [
            p + x[i : i + ROWS, :] * mine + x[HALF + i : HALF + i + ROWS, :] * other for p, x in zip(parts, fields)
        ]
        if keep is not None:
            keep[i : i + ROWS, :] = mine
            send[i : i + ROWS, :] = other.astype(BF16)
    values = [total(p) for p in parts]
    if keep is None:
        rows = [jnp.broadcast_to(x, (1, 128)) for x in values]
        send[...] = jnp.concatenate(rows + [known[0:3, :] * 0.125, jnp.zeros((3, 128), F32)], axis=0)
    else:
        send[HALF:MSG, :] = triple(values)


def first_kernel(*refs):
    table = refs[0]
    groups = refs[1:9]
    x_own, left, right, left2, right2 = refs[9:14]
    state, v_own, xs, known, keep, send, acc = refs[14:]
    norm = sector_sums(table[0], groups)[0] / ENTRIES
    scale = 1.0 / jnp.sqrt(norm + EPS)
    state[0:1, :] = jnp.broadcast_to(norm * scale * scale, (1, 128))
    state[1:8, :] = jnp.zeros((7, 128), F32)
    known[...] = jnp.zeros_like(known)
    for i in range(0, W, ROWS):
        v_own[i : i + ROWS, :] = x_own[i : i + ROWS, :] * scale

    def chunk(index, r, k, row):
        vector = groups[index][pl.ds(k * MSG + row, ROWS), :].astype(F32) * scale
        xs[r, pl.ds(row, ROWS), :] = vector.astype(BF16)

    each_chunk(groups, chunk)
    contract(table, ((left, right), (left2, right2)), xs, acc)
    emit(table[0], acc, v_own, None, known, keep, send)


def step_scalars(state, sums):
    vz, dz, vd, dd, dw = [s / ENTRIES for s in sums[:5]]
    vv, vw = state[0:1, 0:1], state[1:2, 0:1]
    along = vd
    inverse = 1.0 / jnp.sqrt(dd - 2.0 * along * vd + along * along * vv + EPS)
    left = inverse * (vz - along * vw)
    right = inverse * (dw - along * vw)
    corner = inverse * inverse * (dz - along * (vz + dw) + along * along * vw)
    coupling = 0.5 * (left + right)
    half_gap = 0.5 * (vw - corner)
    ritz = 0.5 * (vw + corner) - jnp.sqrt(half_gap * half_gap + coupling * coupling)
    weight_old = corner - ritz
    alpha = weight_old + coupling * inverse * along
    beta = -coupling * inverse
    norm = alpha * alpha * vv + 2.0 * alpha * beta * vd + beta * beta * dd
    factor = 1.0 / jnp.sqrt(norm + EPS)
    alpha, beta = alpha * factor, beta * factor
    new_vv = norm * factor * factor
    theta = alpha * alpha * vw + alpha * beta * (vz + dw) + beta * beta * dz
    return alpha, beta, new_vv, theta, ritz


def step_kernel(first, *refs):
    table = refs[0]
    groups, q_groups = refs[1:9], refs[9:17]
    other_z, q_own, left, right, left2, right2, old_state, old_v_own, old_xs = refs[17:26]
    old_w_own, old_d_own, old_v, old_w = [None] * 4 if first else refs[26:30]
    state, v_own, w_own, d_own, v, w, xs, known, *sent, acc = refs[26 if first else 30 :]
    sums = sector_sums(table[0], groups)
    if first:
        theta = sums[0] / ENTRIES
        state[...] = old_state[...]
    else:
        alpha, beta, new_vv, theta, ritz = step_scalars(old_state, sums)
        state[0:1, :] = jnp.broadcast_to(new_vv, (1, 128))
        state[2:7, :] = old_state[3:8, :]
        state[7:8, :] = jnp.broadcast_to(ritz, (1, 128))
    state[1:2, :] = jnp.broadcast_to(theta, (1, 128))

    def own_chunk(half, ref, i, parts):
        row = pl.multiple_of(i * ROWS, ROWS)
        at = pl.ds(pl.multiple_of(half + row, ROWS), ROWS)
        z = ref[pl.ds(row, ROWS), :].astype(F32)
        if first:
            vector, image = old_v_own[at, :], z
        else:
            vector = alpha * old_v_own[at, :] + beta * old_d_own[at, :]
            image = alpha * old_w_own[at, :] + beta * z
        direct = (image - theta * vector) * q_own[at, :]
        v_own[at, :] = vector
        w_own[at, :] = image
        d_own[at, :] = direct
        return tuple(p + direct * x for p, x in zip(parts, (vector, direct, image)))

    parts = tuple(jnp.zeros((ROWS, W), F32) for _ in range(3))
    for half, ref in ((0, groups[0]), (HALF, other_z)):
        parts = lax.fori_loop(0, HALF // ROWS, functools.partial(own_chunk, half, ref), parts)
    known[...] = jnp.concatenate(
        [jnp.broadcast_to(total(p), (1, 128)) for p in parts] + [jnp.zeros((5, 128), F32)], axis=0
    )

    def chunk(index, r, k, row):
        at = pl.ds(row, ROWS)
        z = groups[index][pl.ds(k * MSG + row, ROWS), :].astype(F32)
        q = q_groups[index][pl.ds(k * HALF + row, ROWS), :].astype(F32)
        if first:
            vector, image = old_xs[r, at, :].astype(F32), z
        else:
            vector = alpha * old_v[r, at, :] + beta * old_xs[r, at, :].astype(F32)
            image = alpha * old_w[r, at, :] + beta * z
        if len(sent) > 1:
            v[r, at, :] = vector
            w[r, at, :] = image
        xs[r, at, :] = ((image - theta * vector) * q).astype(BF16)

    each_chunk(groups, chunk)
    contract(table, ((left, right), (left2, right2)), xs, acc)
    emit(table[0], acc, v_own, d_own, known, *([None] * (2 - len(sent)) + sent))


def pair_sums(chip, mine, came):
    both = sums_of(mine.astype(F32) + came.astype(F32))
    return triple([jnp.where(chip == k // 2, both[k % 2], 0.0) for k in range(8)])


def pair_kernel(chip, keep, send, came, out):
    out[0:HALF, :] = (keep[...] + came[0:HALF, :].astype(F32)).astype(BF16)
    out[HALF:MSG, :] = pair_sums(chip[0], send[HALF:MSG, :], came[HALF:MSG, :])


def two_kernel(own, came, out):
    out[...] = (own[...].astype(F32) + came[...].astype(F32)).astype(BF16)


def chip_sums(tile, known):
    at = sums_of(tile)
    vz, dz = (at[k] + at[k + 2] + at[k + 4] + at[k + 6] for k in (0, 1))
    return [vz, dz] + [known[k : k + 1, 0:1] for k in range(3)]


def four_kernel(own, came, known, out):
    z = own[...].astype(F32) + came[...].astype(F32)
    out[0:HALF, :] = z[0:HALF].astype(BF16)
    out[HALF:MSG, :] = triple(chip_sums(z[HALF:MSG], known))


def last_kernel(core, sums, old_state, v_own, d_own, vector, ritz, turned):
    c = core[0]
    alpha, beta, _, _, lowest = step_scalars(old_state, [sums[k : k + 1, 0:1] for k in range(5)])
    ritz[0:7, :] = old_state[1:8, :]
    ritz[7:8, :] = jnp.broadcast_to(lowest, (1, 128))
    here, there = pl.multiple_of(c * HALF, HALF), pl.multiple_of((1 - c) * HALF, HALF)
    turned[pl.ds(here, HALF), :] = alpha * v_own[0:HALF, :] + beta * d_own[0:HALF, :]
    turned[pl.ds(there, HALF), :] = alpha * v_own[HALF:W, :] + beta * d_own[HALF:W, :]
    vector[...] = jnp.transpose(turned[...])


def shape(*dims, dtype=F32):
    return jax.ShapeDtypeStruct(dims, dtype)


def routes(*masks):
    both = [masks[0], masks[-1]]

    def run(x):
        term, sector = lax.axis_size("term"), lax.axis_size("sector")
        perm = []
        for t in range(term):
            for s in range(sector):
                dt, ds = both[t % 2]
                perm.append((t * sector + s, (t ^ dt) * sector + (s ^ ds)))
        return lax.ppermute(x, ("term", "sector"), perm)

    return run


PAIR = routes((1, 0))
CHIP_A, CHIP_B = routes((2, 0), (6, 0)), routes((6, 0), (2, 0))
INNER = {k: routes((0, 4 * k), (0, k)) for k in (1, 2, 3)}
OUTER = {k: routes((0, k), (0, 4 * k)) for k in (1, 2, 3)}


def gather_blocks(msg):
    low = jnp.concatenate([msg, INNER[1](msg)], axis=0)
    high = jnp.concatenate([INNER[3](msg), INNER[2](msg)], axis=0)
    one_low, three_low = OUTER[1](low), OUTER[3](low)
    one_high, three_high = OUTER[1](high), OUTER[3](high)
    return low, high, one_low, one_high, three_low, three_high, OUTER[1](three_low), OUTER[3](one_high)


def shards(start_vector, precond, op_left, op_right, slot_source, slot_count):
    left, right = op_left[0, 0], op_right[0, 0]
    slots = left.shape[0]
    me = lax.axis_index("sector")
    term = lax.axis_index("term")
    c, x = term % 2, term // 2
    core, chip = c[None].astype(jnp.int32), x[None].astype(jnp.int32)

    sources = slot_source[0, 0] ^ me
    mine = jnp.concatenate([sources, slot_count[0]])
    theirs = PAIR(mine)
    table = jnp.concatenate([mine, theirs])
    is_source = jnp.arange(table.shape[0]) % (slots + 1) < slots
    turned = (table >> 2) | ((table & 3) << 2)
    table = jnp.concatenate([core, jnp.where((c == 0) & is_source, turned, table)])
    half = functools.partial(shape, W, slots * HALF, dtype=BF16)
    right_here, right_there = kernel_call(halves_kernel, [half(), half()], [SM, VM])(core, right)
    left2, right2 = kernel_call(
        settle_kernel,
        [shape(slots, W, W, dtype=BF16), half()],
        [ANY, ANY],
        [pltpu.SemaphoreType.DMA((2,))],
    )(PAIR(left), PAIR(right_there))
    ops = (left, right_here, left2, right2)

    x_own, q_own, msg, q_msg = kernel_call(
        prep_kernel,
        [shape(W, W), shape(W, W), shape(MSG, W, dtype=BF16), shape(HALF, W, dtype=BF16)],
        [SM, VM, VM],
        [pltpu.VMEM((W, W), F32)] * 2,
    )(core, start_vector[0], precond[0])
    groups = gather_blocks(msg)
    q_groups = gather_blocks(q_msg)

    field = functools.partial(shape, SECTORS, HALF, W)
    message = shape(MSG, W, dtype=BF16)
    outs = [shape(8, 128), shape(HALF, W), message]
    acc = [pltpu.VMEM((W, W), F32)]
    state, v_own, xs, known, *sent = kernel_call(
        first_kernel,
        [shape(8, 128), shape(W, W), field(dtype=BF16)] + outs,
        [SM] + [VM] * 13,
        acc,
    )(table, *groups, x_own, *ops)
    older = ()

    for iteration in range(ITERS):
        both = kernel_call(pair_kernel, message, [SM] + [VM] * 3)(chip, *sent, PAIR(sent[1]))
        two = kernel_call(two_kernel, message, [VM] * 2)(both, CHIP_A(both))
        msg = kernel_call(four_kernel, message, [VM] * 3)(two, CHIP_B(two), known)
        other_z = PAIR(msg)
        groups = gather_blocks(msg)
        if iteration + 1 == ITERS:
            outs = [shape(8, 128), shape(8, 128)]
        aliases = {23: 0, 24: 1, 25: 6}
        state, v_own, w_own, d_own, v, w, xs, known, *sent = kernel_call(
            functools.partial(step_kernel, iteration == 0),
            [shape(8, 128), shape(W, W), shape(W, W), shape(W, W), field(), field(), field(dtype=BF16)] + outs,
            [SM] + [VM] * (25 + len(older)),
            acc,
            aliases if iteration == 0 else aliases | {26: 2, 27: 3, 28: 4, 29: 5},
        )(table, *groups, *q_groups, other_z, q_own, *ops, state, v_own, xs, *older)
        older = (w_own, d_own, v, w)

    (sums,) = sent
    for masks in ((1, 0), (2, 0), (6, 0), (0, 1), (0, 3), (0, 4), (0, 12)):
        sums = sums + routes(masks)(sums)
    vector, ritz = kernel_call(
        last_kernel,
        [shape(W, W), shape(8, 128)],
        [SM] + [VM] * 4,
        [pltpu.VMEM((W, W), F32)],
    )(core, sums, state, v_own, d_own)
    return vector[None], ritz[8 - ITERS :, 0]


def solution(mesh):
    in_specs = (
        P("sector", None, None),
        P("sector", None, None),
        P("term", "sector", None, None, None),
        P("term", "sector", None, None, None),
        P("term", "sector", None),
        P("term", "sector"),
    )
    out_specs = (P("sector", None, None), P())
    return jax.shard_map(shards, mesh=mesh, in_specs=in_specs, out_specs=out_specs, check_vma=False)
```

```python
import functools

import jax
import jax.numpy as jnp
from jax import lax
from jax.experimental import pallas as pl
from jax.experimental.pallas import tpu as pltpu
from jax.sharding import PartitionSpec as P


ITERS = 4
EPS = 1e-6
W = 384
HALF = W // 2
SC = 16
MSG = HALF + SC
SECTORS = 16
GROUP = 4
ROWS = 32
ENTRIES = float(SECTORS * W * W)
F32 = jnp.float32
BF16 = jnp.bfloat16
VM = pl.BlockSpec(memory_space=pltpu.VMEM)
SM = pl.BlockSpec(memory_space=pltpu.SMEM)
ANY = pl.BlockSpec(memory_space=pl.ANY)
PARAMS = pltpu.CompilerParams(vmem_limit_bytes=6 * 1024 * 1024)


def kernel_call(body, out_shape, in_specs, scratch=(), aliases=None):
    call = pl.pallas_call(
        body,
        out_shape=jax.tree.map(lambda s: pltpu.VMEM(s.shape, s.dtype), out_shape),
        in_specs=in_specs,
        out_specs=jax.tree.map(lambda _: VM, out_shape),
        scratch_shapes=scratch,
        input_output_aliases=aliases or {},
        compiler_params=PARAMS,
    )

    def run(*operands):
        placed = [
            pltpu.with_memory_space_constraint(x, pltpu.VMEM) if spec is VM else x
            for x, spec in zip(operands, in_specs)
        ]
        return call(*placed)

    return run


def triple(values):
    tall = jnp.concatenate(
        [jnp.broadcast_to(v, (1, 128)) for v in values] + [jnp.zeros((SC - len(values), 128), F32)], axis=0
    )
    high = tall.astype(BF16)
    rest = tall - high.astype(F32)
    mid = rest.astype(BF16)
    low = (rest - mid.astype(F32)).astype(BF16)
    return jnp.concatenate([high, mid, low], axis=1)


def sums_of(tile):
    tall = tile[:, 0:128] + tile[:, 128:256] + tile[:, 256:384]
    return [tall[k : k + 1, 0:1] for k in range(8)]


def total(x):
    return jnp.sum(jnp.sum(x, axis=0, keepdims=True), axis=1, keepdims=True)


def places_of(index):
    outer, high = (0, 0, 1, 1, 3, 3, 2, 2)[index], index % 2
    return (4 * outer + 3, -1) if high else (4 * outer, 1)


def sector_sums(core, groups):
    found = {}
    for index, ref in enumerate(groups):
        base, step = places_of(index)
        for k in (0, 1):
            found[base + step * k] = ref[k * MSG + HALF : (k + 1) * MSG, :].astype(F32)
    straight = core == 1
    tiles = {r: jnp.where(straight, found[r], found[(r >> 2) | ((r & 3) << 2)]) for r in range(SECTORS)}
    for bit in (1, 2, 4, 8):
        tiles = {r: t + tiles[r ^ bit] for r, t in tiles.items() if not r & bit}
    return sums_of(tiles[0])


def each_chunk(groups, body):
    for index in range(len(groups)):
        base, step = places_of(index)
        for k in (0, 1):

            def chunk(i, carry, index=index, r=base + step * k, k=k):
                body(index, r, k, pl.multiple_of(i * ROWS, ROWS))
                return carry

            lax.fori_loop(0, HALF // ROWS, chunk, 0, unroll=True)


def prep_kernel(core, start, precond, x_own, q_own, msg, q_msg, xt, qt):
    c = core[0]
    xt[...] = jnp.transpose(start[...])
    qt[...] = 1.0 / jnp.transpose(precond[...])
    here, there = pl.multiple_of(c * HALF, HALF), pl.multiple_of((1 - c) * HALF, HALF)
    x_own[0:HALF, :] = xt[pl.ds(here, HALF), :]
    x_own[HALF:W, :] = xt[pl.ds(there, HALF), :]
    q_own[0:HALF, :] = qt[pl.ds(here, HALF), :]
    q_own[HALF:W, :] = qt[pl.ds(there, HALF), :]
    x = x_own[...]
    msg[0:HALF, :] = x[0:HALF].astype(BF16)
    msg[HALF:MSG, :] = triple([total(x * x)])
    q_msg[...] = q_own[0:HALF, :].astype(BF16)


def halves_kernel(core, right, here, there):
    straight = core[0] == 0

    def cut(j, carry):
        one, two = right[2 * j], right[2 * j + 1]
        low = jnp.concatenate([one[:, :HALF], two[:, :HALF]], axis=1)
        high = jnp.concatenate([one[:, HALF:], two[:, HALF:]], axis=1)
        at = pl.ds(pl.multiple_of(j * W, W), W)
        here[:, at] = jnp.where(straight, low, high)
        there[:, at] = jnp.where(straight, high, low)
        return carry

    lax.fori_loop(0, right.shape[0] // 2, cut, 0)


def settle_kernel(left, right, left_out, right_out, sems):
    copies = [
        pltpu.make_async_copy(left, left_out, sems.at[0]),
        pltpu.make_async_copy(right, right_out, sems.at[1]),
    ]
    for copy in copies:
        copy.start()
    for copy in copies:
        copy.wait()


def contract(table, ops, xs, acc):
    acc[...] = jnp.zeros_like(acc)
    for index, (left, right) in enumerate(ops):
        slots = left.shape[0]
        first = 1 + index * (slots + 1)
        live = table[first + slots]

        def join(start, size, masked):
            products = []
            for k in range(size):
                slot = start + k
                product = lax.dot_general(
                    xs[table[first + slot]], left[slot], (((1,), (1,)), ((), ())), preferred_element_type=F32
                )
                if masked and k:
                    product = jnp.where(slot < live, product, 0.0)
                products.append(product.astype(BF16))
            at = pl.ds(pl.multiple_of(start * HALF, 2 * HALF), size * HALF)
            acc[...] += jnp.dot(right[:, at], jnp.concatenate(products, axis=0), preferred_element_type=F32)

        def group(j, carry):
            join(j * GROUP, GROUP, False)
            return carry

        whole = live // GROUP
        lax.fori_loop(0, whole, group, 0)
        rest = live - whole * GROUP

        @pl.when(rest > GROUP // 2)
        def _():
            join(whole * GROUP, GROUP, True)

        @pl.when((rest > 0) & (rest <= GROUP // 2))
        def _():
            join(whole * GROUP, GROUP // 2, True)


def emit(c, acc, v_own, d_own, known, keep, send):
    here, there = c * HALF, (1 - c) * HALF
    fields = [x for x in (v_own, d_own) if x is not None]
    parts = [jnp.zeros((ROWS, W), F32) for _ in fields]
    for i in range(0, HALF, ROWS):
        mine = acc[pl.ds(pl.multiple_of(here + i, ROWS), ROWS), :]
        other = acc[pl.ds(pl.multiple_of(there + i, ROWS), ROWS), :]
        parts = [
            p + x[i : i + ROWS, :] * mine + x[HALF + i : HALF + i + ROWS, :] * other for p, x in zip(parts, fields)
        ]
        if keep is not None:
            keep[i : i + ROWS, :] = mine
            send[i : i + ROWS, :] = other.astype(BF16)
    values = [total(p) for p in parts]
    if keep is None:
        rows = [jnp.broadcast_to(x, (1, 128)) for x in values]
        send[...] = jnp.concatenate(rows + [known[0:3, :] * 0.125, jnp.zeros((3, 128), F32)], axis=0)
    else:
        send[HALF:MSG, :] = triple(values)


def first_kernel(*refs):
    table = refs[0]
    groups = refs[1:9]
    x_own, left, right, left2, right2 = refs[9:14]
    state, v_own, xs, known, keep, send, acc = refs[14:]
    norm = sector_sums(table[0], groups)[0] / ENTRIES
    scale = 1.0 / jnp.sqrt(norm + EPS)
    state[0:1, :] = jnp.broadcast_to(norm * scale * scale, (1, 128))
    state[1:8, :] = jnp.zeros((7, 128), F32)
    known[...] = jnp.zeros_like(known)
    for i in range(0, W, ROWS):
        v_own[i : i + ROWS, :] = x_own[i : i + ROWS, :] * scale

    def chunk(index, r, k, row):
        vector = groups[index][pl.ds(k * MSG + row, ROWS), :].astype(F32) * scale
        xs[r, pl.ds(row, ROWS), :] = vector.astype(BF16)

    each_chunk(groups, chunk)
    contract(table, ((left, right), (left2, right2)), xs, acc)
    emit(table[0], acc, v_own, None, known, keep, send)


def step_scalars(state, sums):
    vz, dz, vd, dd, dw = [s / ENTRIES for s in sums[:5]]
    vv, vw = state[0:1, 0:1], state[1:2, 0:1]
    along = vd
    inverse = 1.0 / jnp.sqrt(dd - 2.0 * along * vd + along * along * vv + EPS)
    left = inverse * (vz - along * vw)
    right = inverse * (dw - along * vw)
    corner = inverse * inverse * (dz - along * (vz + dw) + along * along * vw)
    coupling = 0.5 * (left + right)
    half_gap = 0.5 * (vw - corner)
    ritz = 0.5 * (vw + corner) - jnp.sqrt(half_gap * half_gap + coupling * coupling)
    weight_old = corner - ritz
    alpha = weight_old + coupling * inverse * along
    beta = -coupling * inverse
    norm = alpha * alpha * vv + 2.0 * alpha * beta * vd + beta * beta * dd
    factor = 1.0 / jnp.sqrt(norm + EPS)
    alpha, beta = alpha * factor, beta * factor
    new_vv = norm * factor * factor
    theta = alpha * alpha * vw + alpha * beta * (vz + dw) + beta * beta * dz
    return alpha, beta, new_vv, theta, ritz


def step_kernel(first, *refs):
    table = refs[0]
    groups, q_groups = refs[1:9], refs[9:17]
    other_z, q_own, left, right, left2, right2, old_state, old_v_own, old_xs = refs[17:26]
    old_w_own, old_d_own, old_v, old_w = [None] * 4 if first else refs[26:30]
    state, v_own, w_own, d_own, v, w, xs, known, *sent, acc = refs[26 if first else 30 :]
    sums = sector_sums(table[0], groups)
    if first:
        theta = sums[0] / ENTRIES
        state[...] = old_state[...]
    else:
        alpha, beta, new_vv, theta, ritz = step_scalars(old_state, sums)
        state[0:1, :] = jnp.broadcast_to(new_vv, (1, 128))
        state[2:7, :] = old_state[3:8, :]
        state[7:8, :] = jnp.broadcast_to(ritz, (1, 128))
    state[1:2, :] = jnp.broadcast_to(theta, (1, 128))

    def own_chunk(half, ref, i, parts):
        row = pl.multiple_of(i * ROWS, ROWS)
        at = pl.ds(pl.multiple_of(half + row, ROWS), ROWS)
        z = ref[pl.ds(row, ROWS), :].astype(F32)
        if first:
            vector, image = old_v_own[at, :], z
        else:
            vector = alpha * old_v_own[at, :] + beta * old_d_own[at, :]
            image = alpha * old_w_own[at, :] + beta * z
        direct = (image - theta * vector) * q_own[at, :]
        v_own[at, :] = vector
        w_own[at, :] = image
        d_own[at, :] = direct
        return tuple(p + direct * x for p, x in zip(parts, (vector, direct, image)))

    parts = tuple(jnp.zeros((ROWS, W), F32) for _ in range(3))
    for half, ref in ((0, groups[0]), (HALF, other_z)):
        parts = lax.fori_loop(0, HALF // ROWS, functools.partial(own_chunk, half, ref), parts)
    known[...] = jnp.concatenate(
        [jnp.broadcast_to(total(p), (1, 128)) for p in parts] + [jnp.zeros((5, 128), F32)], axis=0
    )

    def chunk(index, r, k, row):
        at = pl.ds(row, ROWS)
        z = groups[index][pl.ds(k * MSG + row, ROWS), :].astype(F32)
        q = q_groups[index][pl.ds(k * HALF + row, ROWS), :].astype(F32)
        if first:
            vector, image = old_xs[r, at, :].astype(F32), z
        else:
            vector = alpha * old_v[r, at, :] + beta * old_xs[r, at, :].astype(F32)
            image = alpha * old_w[r, at, :] + beta * z
        if len(sent) > 1:
            v[r, at, :] = vector
            w[r, at, :] = image
        xs[r, at, :] = ((image - theta * vector) * q).astype(BF16)

    each_chunk(groups, chunk)
    contract(table, ((left, right), (left2, right2)), xs, acc)
    emit(table[0], acc, v_own, d_own, known, *([None] * (2 - len(sent)) + sent))


def pair_sums(chip, mine, came):
    both = sums_of(mine.astype(F32) + came.astype(F32))
    return triple([jnp.where(chip == k // 2, both[k % 2], 0.0) for k in range(8)])


def pair_kernel(chip, keep, send, came, out):
    out[0:HALF, :] = (keep[...] + came[0:HALF, :].astype(F32)).astype(BF16)
    out[HALF:MSG, :] = pair_sums(chip[0], send[HALF:MSG, :], came[HALF:MSG, :])


def two_kernel(own, came, out):
    out[...] = (own[...].astype(F32) + came[...].astype(F32)).astype(BF16)


def chip_sums(tile, known):
    at = sums_of(tile)
    vz, dz = (at[k] + at[k + 2] + at[k + 4] + at[k + 6] for k in (0, 1))
    return [vz, dz] + [known[k : k + 1, 0:1] for k in range(3)]


def four_kernel(own, came, known, out):
    z = own[...].astype(F32) + came[...].astype(F32)
    out[0:HALF, :] = z[0:HALF].astype(BF16)
    out[HALF:MSG, :] = triple(chip_sums(z[HALF:MSG], known))


def last_kernel(core, sums, old_state, v_own, d_own, vector, ritz, turned):
    c = core[0]
    alpha, beta, _, _, lowest = step_scalars(old_state, [sums[k : k + 1, 0:1] for k in range(5)])
    ritz[0:7, :] = old_state[1:8, :]
    ritz[7:8, :] = jnp.broadcast_to(lowest, (1, 128))
    here, there = pl.multiple_of(c * HALF, HALF), pl.multiple_of((1 - c) * HALF, HALF)
    turned[pl.ds(here, HALF), :] = alpha * v_own[0:HALF, :] + beta * d_own[0:HALF, :]
    turned[pl.ds(there, HALF), :] = alpha * v_own[HALF:W, :] + beta * d_own[HALF:W, :]
    vector[...] = jnp.transpose(turned[...])


def shape(*dims, dtype=F32):
    return jax.ShapeDtypeStruct(dims, dtype)


def routes(*masks):
    both = [masks[0], masks[-1]]

    def run(x):
        term, sector = lax.axis_size("term"), lax.axis_size("sector")
        perm = []
        for t in range(term):
            for s in range(sector):
                dt, ds = both[t % 2]
                perm.append((t * sector + s, (t ^ dt) * sector + (s ^ ds)))
        return lax.ppermute(x, ("term", "sector"), perm)

    return run


PAIR = routes((1, 0))
CHIP_A, CHIP_B = routes((2, 0), (6, 0)), routes((6, 0), (2, 0))
INNER = {k: routes((0, 4 * k), (0, k)) for k in (1, 2, 3)}
OUTER = {k: routes((0, k), (0, 4 * k)) for k in (1, 2, 3)}


def gather_blocks(msg):
    low = jnp.concatenate([msg, INNER[1](msg)], axis=0)
    high = jnp.concatenate([INNER[3](msg), INNER[2](msg)], axis=0)
    one_low, three_low = OUTER[1](low), OUTER[3](low)
    one_high, three_high = OUTER[1](high), OUTER[3](high)
    return low, high, one_low, one_high, three_low, three_high, OUTER[1](three_low), OUTER[3](one_high)


def shards(start_vector, precond, op_left, op_right, slot_source, slot_count):
    left, right = op_left[0, 0], op_right[0, 0]
    slots = left.shape[0]
    me = lax.axis_index("sector")
    term = lax.axis_index("term")
    c, x = term % 2, term // 2
    core, chip = c[None].astype(jnp.int32), x[None].astype(jnp.int32)

    sources = slot_source[0, 0] ^ me
    mine = jnp.concatenate([sources, slot_count[0]])
    theirs = PAIR(mine)
    table = jnp.concatenate([mine, theirs])
    is_source = jnp.arange(table.shape[0]) % (slots + 1) < slots
    turned = (table >> 2) | ((table & 3) << 2)
    table = jnp.concatenate([core, jnp.where((c == 0) & is_source, turned, table)])
    half = functools.partial(shape, W, slots * HALF, dtype=BF16)
    right_here, right_there = kernel_call(halves_kernel, [half(), half()], [SM, VM])(core, right)
    left2, right2 = kernel_call(
        settle_kernel,
        [shape(slots, W, W, dtype=BF16), half()],
        [ANY, ANY],
        [pltpu.SemaphoreType.DMA((2,))],
    )(PAIR(left), PAIR(right_there))
    ops = (left, right_here, left2, right2)

    x_own, q_own, msg, q_msg = kernel_call(
        prep_kernel,
        [shape(W, W), shape(W, W), shape(MSG, W, dtype=BF16), shape(HALF, W, dtype=BF16)],
        [SM, VM, VM],
        [pltpu.VMEM((W, W), F32)] * 2,
    )(core, start_vector[0], precond[0])
    groups = gather_blocks(msg)
    q_groups = gather_blocks(q_msg)

    field = functools.partial(shape, SECTORS, HALF, W)
    message = shape(MSG, W, dtype=BF16)
    outs = [shape(8, 128), shape(HALF, W), message]
    acc = [pltpu.VMEM((W, W), F32)]
    state, v_own, xs, known, *sent = kernel_call(
        first_kernel,
        [shape(8, 128), shape(W, W), field(dtype=BF16)] + outs,
        [SM] + [VM] * 13,
        acc,
    )(table, *groups, x_own, *ops)
    older = ()

    for iteration in range(ITERS):
        both = kernel_call(pair_kernel, message, [SM] + [VM] * 3)(chip, *sent, PAIR(sent[1]))
        two = kernel_call(two_kernel, message, [VM] * 2)(both, CHIP_A(both))
        msg = kernel_call(four_kernel, message, [VM] * 3)(two, CHIP_B(two), known)
        other_z = PAIR(msg)
        groups = gather_blocks(msg)
        if iteration + 1 == ITERS:
            outs = [shape(8, 128), shape(8, 128)]
        aliases = {23: 0, 24: 1, 25: 6}
        state, v_own, w_own, d_own, v, w, xs, known, *sent = kernel_call(
            functools.partial(step_kernel, iteration == 0),
            [shape(8, 128), shape(W, W), shape(W, W), shape(W, W), field(), field(), field(dtype=BF16)] + outs,
            [SM] + [VM] * (25 + len(older)),
            acc,
            aliases if iteration == 0 else aliases | {26: 2, 27: 3, 28: 4, 29: 5},
        )(table, *groups, *q_groups, other_z, q_own, *ops, state, v_own, xs, *older)
        older = (w_own, d_own, v, w)

    (sums,) = sent
    for masks in ((1, 0), (2, 0), (6, 0), (0, 1), (0, 3), (0, 4), (0, 12)):
        sums = sums + routes(masks)(sums)
    vector, ritz = kernel_call(
        last_kernel,
        [shape(W, W), shape(8, 128)],
        [SM] + [VM] * 4,
        [pltpu.VMEM((W, W), F32)],
    )(core, sums, state, v_own, d_own)
    return vector[None], ritz[8 - ITERS :, 0]


def solution(mesh):
    in_specs = (
        P("sector", None, None),
        P("sector", None, None),
        P("term", "sector", None, None, None),
        P("term", "sector", None, None, None),
        P("term", "sector", None),
        P("term", "sector"),
    )
    out_specs = (P("sector", None, None), P())
    return jax.shard_map(shards, mesh=mesh, in_specs=in_specs, out_specs=out_specs, check_vma=False)
```

```python
import functools

import jax
import jax.numpy as jnp
from jax import lax
from jax.experimental import pallas as pl
from jax.experimental.pallas import tpu as pltpu
from jax.sharding import PartitionSpec as P


ITERS = 4
EPS = 1e-6
W = 384
HALF = W // 2
SC = 16
MSG = HALF + SC
SECTORS = 16
GROUP = 4
ROWS = 32
ENTRIES = float(SECTORS * W * W)
F32 = jnp.float32
BF16 = jnp.bfloat16
VM = pl.BlockSpec(memory_space=pltpu.VMEM)
SM = pl.BlockSpec(memory_space=pltpu.SMEM)
ANY = pl.BlockSpec(memory_space=pl.ANY)
PARAMS = pltpu.CompilerParams(vmem_limit_bytes=6 * 1024 * 1024)


def kernel_call(body, out_shape, in_specs, scratch=(), aliases=None):
    call = pl.pallas_call(
        body,
        out_shape=jax.tree.map(lambda s: pltpu.VMEM(s.shape, s.dtype), out_shape),
        in_specs=in_specs,
        out_specs=jax.tree.map(lambda _: VM, out_shape),
        scratch_shapes=scratch,
        input_output_aliases=aliases or {},
        compiler_params=PARAMS,
    )

    def run(*operands):
        placed = [
            pltpu.with_memory_space_constraint(x, pltpu.VMEM) if spec is VM else x
            for x, spec in zip(operands, in_specs)
        ]
        return call(*placed)

    return run


def triple(values):
    tall = jnp.concatenate(
        [jnp.broadcast_to(v, (1, 128)) for v in values] + [jnp.zeros((SC - len(values), 128), F32)], axis=0
    )
    high = tall.astype(BF16)
    rest = tall - high.astype(F32)
    mid = rest.astype(BF16)
    low = (rest - mid.astype(F32)).astype(BF16)
    return jnp.concatenate([high, mid, low], axis=1)


def sums_of(tile):
    tall = tile[:, 0:128] + tile[:, 128:256] + tile[:, 256:384]
    return [tall[k : k + 1, 0:1] for k in range(8)]


def total(x):
    return jnp.sum(jnp.sum(x, axis=0, keepdims=True), axis=1, keepdims=True)


def places_of(index):
    outer, high = (0, 0, 1, 1, 3, 3, 2, 2)[index], index % 2
    return (4 * outer + 3, -1) if high else (4 * outer, 1)


def sector_sums(core, groups):
    found = {}
    for index, ref in enumerate(groups):
        base, step = places_of(index)
        for k in (0, 1):
            found[base + step * k] = ref[k * MSG + HALF : (k + 1) * MSG, :].astype(F32)
    straight = core == 1
    tiles = {r: jnp.where(straight, found[r], found[(r >> 2) | ((r & 3) << 2)]) for r in range(SECTORS)}
    for bit in (1, 2, 4, 8):
        tiles = {r: t + tiles[r ^ bit] for r, t in tiles.items() if not r & bit}
    return sums_of(tiles[0])


def each_chunk(groups, body):
    for index in range(len(groups)):
        base, step = places_of(index)
        for k in (0, 1):

            def chunk(i, carry, index=index, r=base + step * k, k=k):
                body(index, r, k, pl.multiple_of(i * ROWS, ROWS))
                return carry

            lax.fori_loop(0, HALF // ROWS, chunk, 0, unroll=True)


def prep_kernel(core, start, precond, x_own, q_own, msg, q_msg, xt, qt):
    c = core[0]
    xt[...] = jnp.transpose(start[...])
    qt[...] = 1.0 / jnp.transpose(precond[...])
    here, there = pl.multiple_of(c * HALF, HALF), pl.multiple_of((1 - c) * HALF, HALF)
    x_own[0:HALF, :] = xt[pl.ds(here, HALF), :]
    x_own[HALF:W, :] = xt[pl.ds(there, HALF), :]
    q_own[0:HALF, :] = qt[pl.ds(here, HALF), :]
    q_own[HALF:W, :] = qt[pl.ds(there, HALF), :]
    x = x_own[...]
    msg[0:HALF, :] = x[0:HALF].astype(BF16)
    msg[HALF:MSG, :] = triple([total(x * x)])
    q_msg[...] = q_own[0:HALF, :].astype(BF16)


def halves_kernel(core, right, here, there):
    straight = core[0] == 0

    def cut(j, carry):
        one, two = right[2 * j], right[2 * j + 1]
        low = jnp.concatenate([one[:, :HALF], two[:, :HALF]], axis=1)
        high = jnp.concatenate([one[:, HALF:], two[:, HALF:]], axis=1)
        at = pl.ds(pl.multiple_of(j * W, W), W)
        here[:, at] = jnp.where(straight, low, high)
        there[:, at] = jnp.where(straight, high, low)
        return carry

    lax.fori_loop(0, right.shape[0] // 2, cut, 0)


def settle_kernel(left, right, left_out, right_out, sems):
    copies = [
        pltpu.make_async_copy(left, left_out, sems.at[0]),
        pltpu.make_async_copy(right, right_out, sems.at[1]),
    ]
    for copy in copies:
        copy.start()
    for copy in copies:
        copy.wait()


def contract(table, ops, xs, acc):
    acc[...] = jnp.zeros_like(acc)
    for index, (left, right) in enumerate(ops):
        slots = left.shape[0]
        first = 1 + index * (slots + 1)
        live = table[first + slots]

        def join(start, size, masked):
            products = []
            for k in range(size):
                slot = start + k
                product = lax.dot_general(
                    xs[table[first + slot]], left[slot], (((1,), (1,)), ((), ())), preferred_element_type=F32
                )
                if masked and k:
                    product = jnp.where(slot < live, product, 0.0)
                products.append(product.astype(BF16))
            at = pl.ds(pl.multiple_of(start * HALF, 2 * HALF), size * HALF)
            acc[...] += jnp.dot(right[:, at], jnp.concatenate(products, axis=0), preferred_element_type=F32)

        def group(j, carry):
            join(j * GROUP, GROUP, False)
            return carry

        whole = live // GROUP
        lax.fori_loop(0, whole, group, 0)
        rest = live - whole * GROUP

        @pl.when(rest > GROUP // 2)
        def _():
            join(whole * GROUP, GROUP, True)

        @pl.when((rest > 0) & (rest <= GROUP // 2))
        def _():
            join(whole * GROUP, GROUP // 2, True)


def emit(c, acc, v_own, d_own, known, keep, send):
    here, there = c * HALF, (1 - c) * HALF
    fields = [x for x in (v_own, d_own) if x is not None]
    parts = [jnp.zeros((ROWS, W), F32) for _ in fields]
    for i in range(0, HALF, ROWS):
        mine = acc[pl.ds(pl.multiple_of(here + i, ROWS), ROWS), :]
        other = acc[pl.ds(pl.multiple_of(there + i, ROWS), ROWS), :]
        parts = [
            p + x[i : i + ROWS, :] * mine + x[HALF + i : HALF + i + ROWS, :] * other for p, x in zip(parts, fields)
        ]
        if keep is not None:
            keep[i : i + ROWS, :] = mine
            send[i : i + ROWS, :] = other.astype(BF16)
    values = [total(p) for p in parts]
    if keep is None:
        rows = [jnp.broadcast_to(x, (1, 128)) for x in values]
        send[...] = jnp.concatenate(rows + [known[0:3, :] * 0.125, jnp.zeros((3, 128), F32)], axis=0)
    else:
        send[HALF:MSG, :] = triple(values)


def first_kernel(*refs):
    table = refs[0]
    groups = refs[1:9]
    x_own, left, right, left2, right2 = refs[9:14]
    state, v_own, xs, known, keep, send, acc = refs[14:]
    norm = sector_sums(table[0], groups)[0] / ENTRIES
    scale = 1.0 / jnp.sqrt(norm + EPS)
    state[0:1, :] = jnp.broadcast_to(norm * scale * scale, (1, 128))
    state[1:8, :] = jnp.zeros((7, 128), F32)
    known[...] = jnp.zeros_like(known)
    for i in range(0, W, ROWS):
        v_own[i : i + ROWS, :] = x_own[i : i + ROWS, :] * scale

    def chunk(index, r, k, row):
        vector = groups[index][pl.ds(k * MSG + row, ROWS), :].astype(F32) * scale
        xs[r, pl.ds(row, ROWS), :] = vector.astype(BF16)

    each_chunk(groups, chunk)
    contract(table, ((left, right), (left2, right2)), xs, acc)
    emit(table[0], acc, v_own, None, known, keep, send)


def step_scalars(state, sums):
    vz, dz, vd, dd, dw = [s / ENTRIES for s in sums[:5]]
    vv, vw = state[0:1, 0:1], state[1:2, 0:1]
    along = vd
    inverse = 1.0 / jnp.sqrt(dd - 2.0 * along * vd + along * along * vv + EPS)
    left = inverse * (vz - along * vw)
    right = inverse * (dw - along * vw)
    corner = inverse * inverse * (dz - along * (vz + dw) + along * along * vw)
    coupling = 0.5 * (left + right)
    half_gap = 0.5 * (vw - corner)
    ritz = 0.5 * (vw + corner) - jnp.sqrt(half_gap * half_gap + coupling * coupling)
    weight_old = corner - ritz
    alpha = weight_old + coupling * inverse * along
    beta = -coupling * inverse
    norm = alpha * alpha * vv + 2.0 * alpha * beta * vd + beta * beta * dd
    factor = 1.0 / jnp.sqrt(norm + EPS)
    alpha, beta = alpha * factor, beta * factor
    new_vv = norm * factor * factor
    theta = alpha * alpha * vw + alpha * beta * (vz + dw) + beta * beta * dz
    return alpha, beta, new_vv, theta, ritz


def step_kernel(first, *refs):
    table = refs[0]
    groups, q_groups = refs[1:9], refs[9:17]
    other_z, q_own, left, right, left2, right2, old_state, old_v_own, old_xs = refs[17:26]
    old_w_own, old_d_own, old_v, old_w = [None] * 4 if first else refs[26:30]
    state, v_own, w_own, d_own, v, w, xs, known, *sent, acc = refs[26 if first else 30 :]
    sums = sector_sums(table[0], groups)
    if first:
        theta = sums[0] / ENTRIES
        state[...] = old_state[...]
    else:
        alpha, beta, new_vv, theta, ritz = step_scalars(old_state, sums)
        state[0:1, :] = jnp.broadcast_to(new_vv, (1, 128))
        state[2:7, :] = old_state[3:8, :]
        state[7:8, :] = jnp.broadcast_to(ritz, (1, 128))
    state[1:2, :] = jnp.broadcast_to(theta, (1, 128))

    def own_chunk(half, ref, i, parts):
        row = pl.multiple_of(i * ROWS, ROWS)
        at = pl.ds(pl.multiple_of(half + row, ROWS), ROWS)
        z = ref[pl.ds(row, ROWS), :].astype(F32)
        if first:
            vector, image = old_v_own[at, :], z
        else:
            vector = alpha * old_v_own[at, :] + beta * old_d_own[at, :]
            image = alpha * old_w_own[at, :] + beta * z
        direct = (image - theta * vector) * q_own[at, :]
        v_own[at, :] = vector
        w_own[at, :] = image
        d_own[at, :] = direct
        return tuple(p + direct * x for p, x in zip(parts, (vector, direct, image)))

    parts = tuple(jnp.zeros((ROWS, W), F32) for _ in range(3))
    for half, ref in ((0, groups[0]), (HALF, other_z)):
        parts = lax.fori_loop(0, HALF // ROWS, functools.partial(own_chunk, half, ref), parts, unroll=True)
    known[...] = jnp.concatenate(
        [jnp.broadcast_to(total(p), (1, 128)) for p in parts] + [jnp.zeros((5, 128), F32)], axis=0
    )

    def chunk(index, r, k, row):
        at = pl.ds(row, ROWS)
        z = groups[index][pl.ds(k * MSG + row, ROWS), :].astype(F32)
        q = q_groups[index][pl.ds(k * HALF + row, ROWS), :].astype(F32)
        if first:
            vector, image = old_xs[r, at, :].astype(F32), z
        else:
            vector = alpha * old_v[r, at, :] + beta * old_xs[r, at, :].astype(F32)
            image = alpha * old_w[r, at, :] + beta * z
        if len(sent) > 1:
            v[r, at, :] = vector
            w[r, at, :] = image
        xs[r, at, :] = ((image - theta * vector) * q).astype(BF16)

    each_chunk(groups, chunk)
    contract(table, ((left, right), (left2, right2)), xs, acc)
    emit(table[0], acc, v_own, d_own, known, *([None] * (2 - len(sent)) + sent))


def pair_sums(chip, mine, came):
    both = sums_of(mine.astype(F32) + came.astype(F32))
    return triple([jnp.where(chip == k // 2, both[k % 2], 0.0) for k in range(8)])


def pair_kernel(chip, keep, send, came, out):
    out[0:HALF, :] = (keep[...] + came[0:HALF, :].astype(F32)).astype(BF16)
    out[HALF:MSG, :] = pair_sums(chip[0], send[HALF:MSG, :], came[HALF:MSG, :])


def two_kernel(own, came, out):
    out[...] = (own[...].astype(F32) + came[...].astype(F32)).astype(BF16)


def chip_sums(tile, known):
    at = sums_of(tile)
    vz, dz = (at[k] + at[k + 2] + at[k + 4] + at[k + 6] for k in (0, 1))
    return [vz, dz] + [known[k : k + 1, 0:1] for k in range(3)]


def four_kernel(own, came, known, out):
    z = own[...].astype(F32) + came[...].astype(F32)
    out[0:HALF, :] = z[0:HALF].astype(BF16)
    out[HALF:MSG, :] = triple(chip_sums(z[HALF:MSG], known))


def last_kernel(core, sums, old_state, v_own, d_own, vector, ritz, turned):
    c = core[0]
    alpha, beta, _, _, lowest = step_scalars(old_state, [sums[k : k + 1, 0:1] for k in range(5)])
    ritz[0:7, :] = old_state[1:8, :]
    ritz[7:8, :] = jnp.broadcast_to(lowest, (1, 128))
    here, there = pl.multiple_of(c * HALF, HALF), pl.multiple_of((1 - c) * HALF, HALF)
    turned[pl.ds(here, HALF), :] = alpha * v_own[0:HALF, :] + beta * d_own[0:HALF, :]
    turned[pl.ds(there, HALF), :] = alpha * v_own[HALF:W, :] + beta * d_own[HALF:W, :]
    vector[...] = jnp.transpose(turned[...])


def shape(*dims, dtype=F32):
    return jax.ShapeDtypeStruct(dims, dtype)


def routes(*masks):
    both = [masks[0], masks[-1]]

    def run(x):
        term, sector = lax.axis_size("term"), lax.axis_size("sector")
        perm = []
        for t in range(term):
            for s in range(sector):
                dt, ds = both[t % 2]
                perm.append((t * sector + s, (t ^ dt) * sector + (s ^ ds)))
        return lax.ppermute(x, ("term", "sector"), perm)

    return run


PAIR = routes((1, 0))
CHIP_A, CHIP_B = routes((2, 0), (6, 0)), routes((6, 0), (2, 0))
INNER = {k: routes((0, 4 * k), (0, k)) for k in (1, 2, 3)}
OUTER = {k: routes((0, k), (0, 4 * k)) for k in (1, 2, 3)}


def gather_blocks(msg):
    low = jnp.concatenate([msg, INNER[1](msg)], axis=0)
    high = jnp.concatenate([INNER[3](msg), INNER[2](msg)], axis=0)
    one_low, three_low = OUTER[1](low), OUTER[3](low)
    one_high, three_high = OUTER[1](high), OUTER[3](high)
    return low, high, one_low, one_high, three_low, three_high, OUTER[1](three_low), OUTER[3](one_high)


def shards(start_vector, precond, op_left, op_right, slot_source, slot_count):
    left, right = op_left[0, 0], op_right[0, 0]
    slots = left.shape[0]
    me = lax.axis_index("sector")
    term = lax.axis_index("term")
    c, x = term % 2, term // 2
    core, chip = c[None].astype(jnp.int32), x[None].astype(jnp.int32)

    sources = slot_source[0, 0] ^ me
    mine = jnp.concatenate([sources, slot_count[0]])
    theirs = PAIR(mine)
    table = jnp.concatenate([mine, theirs])
    is_source = jnp.arange(table.shape[0]) % (slots + 1) < slots
    turned = (table >> 2) | ((table & 3) << 2)
    table = jnp.concatenate([core, jnp.where((c == 0) & is_source, turned, table)])
    half = functools.partial(shape, W, slots * HALF, dtype=BF16)
    right_here, right_there = kernel_call(halves_kernel, [half(), half()], [SM, VM])(core, right)
    left2, right2 = kernel_call(
        settle_kernel,
        [shape(slots, W, W, dtype=BF16), half()],
        [ANY, ANY],
        [pltpu.SemaphoreType.DMA((2,))],
    )(PAIR(left), PAIR(right_there))
    ops = (left, right_here, left2, right2)

    x_own, q_own, msg, q_msg = kernel_call(
        prep_kernel,
        [shape(W, W), shape(W, W), shape(MSG, W, dtype=BF16), shape(HALF, W, dtype=BF16)],
        [SM, VM, VM],
        [pltpu.VMEM((W, W), F32)] * 2,
    )(core, start_vector[0], precond[0])
    groups = gather_blocks(msg)
    q_groups = gather_blocks(q_msg)

    field = functools.partial(shape, SECTORS, HALF, W)
    message = shape(MSG, W, dtype=BF16)
    outs = [shape(8, 128), shape(HALF, W), message]
    acc = [pltpu.VMEM((W, W), F32)]
    state, v_own, xs, known, *sent = kernel_call(
        first_kernel,
        [shape(8, 128), shape(W, W), field(dtype=BF16)] + outs,
        [SM] + [VM] * 13,
        acc,
    )(table, *groups, x_own, *ops)
    older = ()

    for iteration in range(ITERS):
        both = kernel_call(pair_kernel, message, [SM] + [VM] * 3)(chip, *sent, PAIR(sent[1]))
        two = kernel_call(two_kernel, message, [VM] * 2)(both, CHIP_A(both))
        msg = kernel_call(four_kernel, message, [VM] * 3)(two, CHIP_B(two), known)
        other_z = PAIR(msg)
        groups = gather_blocks(msg)
        if iteration + 1 == ITERS:
            outs = [shape(8, 128), shape(8, 128)]
        aliases = {23: 0, 24: 1, 25: 6}
        state, v_own, w_own, d_own, v, w, xs, known, *sent = kernel_call(
            functools.partial(step_kernel, iteration == 0),
            [shape(8, 128), shape(W, W), shape(W, W), shape(W, W), field(), field(), field(dtype=BF16)] + outs,
            [SM] + [VM] * (25 + len(older)),
            acc,
            aliases if iteration == 0 else aliases | {26: 2, 27: 3, 28: 4, 29: 5},
        )(table, *groups, *q_groups, other_z, q_own, *ops, state, v_own, xs, *older)
        older = (w_own, d_own, v, w)

    (sums,) = sent
    for masks in ((1, 0), (2, 0), (6, 0), (0, 1), (0, 3), (0, 4), (0, 12)):
        sums = sums + routes(masks)(sums)
    vector, ritz = kernel_call(
        last_kernel,
        [shape(W, W), shape(8, 128)],
        [SM] + [VM] * 4,
        [pltpu.VMEM((W, W), F32)],
    )(core, sums, state, v_own, d_own)
    return vector[None], ritz[8 - ITERS :, 0]


def solution(mesh):
    in_specs = (
        P("sector", None, None),
        P("sector", None, None),
        P("term", "sector", None, None, None),
        P("term", "sector", None, None, None),
        P("term", "sector", None),
        P("term", "sector"),
    )
    out_specs = (P("sector", None, None), P())
    return jax.shard_map(shards, mesh=mesh, in_specs=in_specs, out_specs=out_specs, check_vma=False)
```
